32 devices in a mesh: req: 4 (over z), row: 2 (over y), col: 4 (over x, core).
Axes of the slice: x: 2, y: 2, z: 4, core: 2. Of those that a mesh axis runs over, the one named last changes fastest.
Arguments:
- tokens: bfloat16 [8192, 2, 1792], P(('req', 'row'), None, 'col'), may hold values from -6 to 6
- w_query: bfloat16 [1792, 256], P('col', 'row'), may hold values from -0.125 to 0.125
- w_key: bfloat16 [1792, 256], P('col', 'row'), may hold values from -0.125 to 0.125
- w_value: bfloat16 [16, 200704], P('row', 'col'), may hold values from -0.125 to 0.125
- w_out: bfloat16 [1792, 1792], P('row', 'col'), may hold values from -0.125 to 0.125
- cached_state: bfloat16 [16, 273, 57344], P(('req', 'col'), None, 'row'), may hold values from -24 to 24
- cached_norm: bfloat16 [512, 273, 16], P(('req', 'col'), None, 'row'), as said below
- slot_prompt: int32 [512], P(('req', 'col')), may hold values from 0 to 511, as said below
- prompt_of: int32 [8192], P(('req', 'col')), may hold values from 0 to 511, as said below
- tail_keys: bfloat16 [8192, 2048], P(('req', 'col'), 'row'), may hold values from -6 to 6
- tail_values: bfloat16 [8192, 14336], P(('req', 'col'), 'row'), may hold values from -6 to 6
- tail_length: int32 [8192], P(('req', 'col')), may hold values from 0 to 8, as said below
Outputs:
- layer_out: bfloat16 [8192, 2, 1792], P(('req', 'row'), None, 'col')
The draws below stay inside these ranges and needn't reach their ends.
Inputs may be any that keep to these rules, and one draw needn't show every extreme that they name: `slot_prompt`: each prompt sits in exactly one slot. The h-th block of 32 slots (holder h) keeps exactly 16 of its own prompts h * 32 to (h + 1) * 32 - 1; its other slots hold prompts of other holders, at most 2 of any one holder. The bound 2 is reached: some holder keeps 2 of one other holder's prompts. `prompt_of`: the h-th aligned block of 512 continuations holds exactly 16 continuations of each prompt h * 32 to (h + 1) * 32 - 1. `tail_length`: each aligned block of 512 continuations holds at least one continuation with a tail of 8 tokens. `cached_norm`: each prompt's column for a head is a sum of phi of some key vectors with positive weights.
All inputs are finite; a program needn't handle non-finite values.
Results may differ from the reference program's by a relative error of at most 0.019.
Values may be sent and summed in bfloat16 or wider, within the bound.
A program may use at most 192 MiB of HBM per device.

```python
import jax
import jax.numpy as jnp
from jax import lax

D = 1792
HEADS = 16
FEAT = 16
HEAD_DIM = 112
QK = 256
TAYLOR = 273
CONTS_PER = 16
P_DEV = 32
TAIL = 8
HOLDERS = 16
PROMPTS = 512
CONT = 8192
N_ROW = 2
N_COL = 4


def holder_table(key):
    half_count = P_DEV // 2
    group_keys = jax.random.split(jax.random.fold_in(key, 11), HOLDERS)
    orders = jax.vmap(lambda subkey: jax.random.permutation(subkey, P_DEV))(group_keys)
    steps_along = jnp.arange(half_count)
    offsets = 1 + (HOLDERS - 2 + steps_along * (HOLDERS // 2)) % (HOLDERS - 1)
    holders = jnp.arange(HOLDERS)
    sources = (holders[:, None] - offsets[None, :]) % HOLDERS
    incoming = sources * P_DEV + orders[sources, half_count + jnp.arange(half_count)[None, :]]
    staying = holders[:, None] * P_DEV + orders[:, :half_count]
    contents = jnp.concatenate([staying, incoming], axis=1)
    shuffle_keys = jax.random.split(jax.random.fold_in(key, 13), HOLDERS)
    shuffles = jax.vmap(lambda subkey: jax.random.permutation(subkey, P_DEV))(shuffle_keys)
    return jnp.take_along_axis(contents, shuffles, axis=1).reshape(-1).astype(jnp.int32)


def draw_slot_prompt(key, part):
    return holder_table(key)


def draw_prompt_of(key, part):
    block_rows = CONTS_PER * P_DEV
    block_keys = jax.random.split(jax.random.fold_in(key, 21), HOLDERS)
    orders = jax.vmap(lambda subkey: jax.random.permutation(subkey, block_rows))(block_keys)
    return (jnp.arange(HOLDERS)[:, None] * P_DEV + orders // CONTS_PER).reshape(-1).astype(jnp.int32)


def draw_tail_length(key, part):
    block_rows = CONTS_PER * P_DEV
    drawn = jax.random.randint(jax.random.fold_in(key, 31), (HOLDERS, block_rows), 0, TAIL + 1)
    longest_at = jax.random.randint(jax.random.fold_in(key, 32), (HOLDERS, 1), 0, block_rows)
    drawn = jnp.where(jnp.arange(block_rows)[None, :] == longest_at, TAIL, drawn)
    return drawn.reshape(-1).astype(jnp.int32)


def draw_cached_norm(key, part):
    pseudo_count = 8
    pseudo_keys = jax.random.normal(jax.random.fold_in(key, 41), (PROMPTS, HEADS, pseudo_count, FEAT), jnp.float32)
    weights = jax.random.uniform(jax.random.fold_in(key, 42), (PROMPTS, HEADS, pseudo_count), jnp.float32, 0.5, 1.5)
    linear = pseudo_keys * FEAT ** (-0.25)
    square = (pseudo_keys[..., :, None] * pseudo_keys[..., None, :]).reshape(PROMPTS, HEADS, pseudo_count, FEAT * FEAT)
    square = square * (0.5 ** 0.5 / FEAT ** 0.5)
    unit_column = jnp.ones((PROMPTS, HEADS, pseudo_count, 1), jnp.float32)
    taylor_terms = jnp.concatenate([unit_column, linear, square], axis=-1)
    weighted = jnp.sum(weights[..., None] * taylor_terms, axis=2)
    return jnp.transpose(weighted, (0, 2, 1)).astype(jnp.bfloat16)


def steps_of(own_key, shape, shards, least, top_value):
    def one(axis_at, parts):
        steps = jax.random.uniform(jax.random.fold_in(jax.random.fold_in(own_key, 6), axis_at), (parts,), jnp.float32, least / len(shards), top_value / len(shards))
        return jnp.repeat(jnp.exp(steps), shape[axis_at] // parts).reshape((-1,) + (1,) * (len(shape) - axis_at - 1))

    level = one(*shards[0])
    for cut in shards[1:]:
        level = level * one(*cut)
    return level


def normal_values(key, shape, deviation, bound, pieces=(), kind=jnp.bfloat16):
    level = steps_of(key, shape, pieces, -0.22, 0.18) if pieces else 1.0
    values = jax.random.normal(key, shape, jnp.float32) * deviation * level
    return jnp.minimum(jnp.maximum(values, -bound), bound).astype(kind)


def setup_inputs(seed: int = 0) -> dict:
    key_list = jax.random.split(jax.random.key(seed), 13)
    return {
        "tokens": normal_values(key_list[0], (CONT, 2, D), 1.0, 6.0, ((0, 8), (2, 4))),
        "w_query": normal_values(key_list[1], (D, QK), D ** -0.5, 0.125, ((0, 4), (1, 2))),
        "w_key": normal_values(key_list[2], (D, QK), D ** -0.5, 0.125, ((0, 4), (1, 2))),
        "w_value": normal_values(key_list[3], (HEADS, D * HEAD_DIM), D ** -0.5, 0.125, ((0, 2), (1, 4))),
        "w_out": normal_values(key_list[4], (D, D), D ** -0.5, 0.125, ((0, 2), (1, 4))),
        "cached_state": normal_values(key_list[5], (HOLDERS, TAYLOR, D * P_DEV), 4.0, 24.0, ((0, 16), (2, 2))),
        "cached_norm": draw_cached_norm(jax.random.fold_in(key_list[12], 71), 0),
        "slot_prompt": draw_slot_prompt(jax.random.fold_in(key_list[12], 71), 0),
        "prompt_of": draw_prompt_of(jax.random.fold_in(key_list[12], 71), 0),
        "tail_keys": normal_values(key_list[9], (CONT, HEADS * TAIL * FEAT), 1.0, 6.0, ((0, 16), (1, 2))),
        "tail_values": normal_values(key_list[10], (CONT, D * TAIL), 1.0, 6.0, ((0, 16), (1, 2))),
        "tail_length": draw_tail_length(jax.random.fold_in(key_list[12], 71), 0),
    }


def features(values):
    feature_width = values.shape[-1]
    linear = values * feature_width ** -0.25
    square = (values[..., :, None] * values[..., None, :]).reshape(values.shape[:-1] + (feature_width * feature_width,))
    square = square * (0.5 ** 0.5 / feature_width ** 0.5)
    unit_column = jnp.ones(values.shape[:-1] + (1,), values.dtype)
    return jnp.concatenate([unit_column, linear, square], axis=-1)


def kernel_weight(scores):
    return 1.0 + scores + 0.5 * scores * scores


def rounded(values):
    return lax.optimization_barrier(values.astype(jnp.bfloat16)).astype(jnp.float32)


def reference(tokens, w_query, w_key, w_value, w_out, cached_state, cached_norm, slot_prompt, prompt_of, tail_keys, tail_values, tail_length):
    highest = lax.Precision.HIGHEST
    value_weight = jnp.transpose(w_value.reshape(HEADS, D, HEAD_DIM), (1, 0, 2)).reshape(D, D)
    stacked = jnp.concatenate([w_query, w_key, value_weight], axis=1).astype(jnp.float32)
    token_values = tokens.astype(jnp.float32)
    col_width = D // N_COL
    summed = jnp.zeros((CONT, 2, stacked.shape[1]), jnp.float32)
    for block_index in range(N_COL):
        lower = block_index * col_width
        product = jnp.einsum("ctd,de->cte", token_values[:, :, lower:lower + col_width], stacked[lower:lower + col_width], precision=highest)
        summed = summed + rounded(product)
    projected = rounded(summed)
    queries = projected[:, :, :QK].reshape(CONT, 2, HEADS, FEAT)
    key_new = projected[:, :, QK:2 * QK].reshape(CONT, 2, HEADS, FEAT)
    value_new = projected[:, :, 2 * QK:].reshape(CONT, 2, HEADS, HEAD_DIM)
    inverse = jnp.argsort(slot_prompt, stable=True).astype(jnp.int32)
    block_rows = CONTS_PER * P_DEV
    scale = FEAT ** -0.5
    causal = (jnp.arange(2)[:, None] >= jnp.arange(2)[None, :]).astype(jnp.float32)
    state_blocks = cached_state.reshape(HOLDERS, TAYLOR, D, P_DEV)

    def one_block(block_index):
        start = (block_index * block_rows).astype(jnp.int32)
        queries_here = lax.dynamic_slice_in_dim(queries, start, block_rows, 0)
        keys_here = lax.dynamic_slice_in_dim(key_new, start, block_rows, 0)
        values_here = lax.dynamic_slice_in_dim(value_new, start, block_rows, 0)
        tail_k = lax.dynamic_slice_in_dim(tail_keys, start, block_rows, 0).astype(jnp.float32).reshape(block_rows, HEADS, TAIL, FEAT)
        tail_v = lax.dynamic_slice_in_dim(tail_values, start, block_rows, 0).astype(jnp.float32).reshape(block_rows, HEADS, TAIL, HEAD_DIM)
        lengths = lax.dynamic_slice_in_dim(tail_length, start, block_rows, 0)
        owner_ids = lax.dynamic_slice_in_dim(prompt_of, start, block_rows, 0)
        slot_index = lax.dynamic_slice_in_dim(inverse, (block_index * P_DEV).astype(jnp.int32), P_DEV, 0)
        holder_of = (slot_index // P_DEV).astype(jnp.int32)
        within = (slot_index % P_DEV).astype(jnp.int32)
        states = state_blocks[holder_of, :, :, within].astype(jnp.float32).reshape(P_DEV, TAYLOR, HEADS, HEAD_DIM)
        norms = cached_norm[slot_index].astype(jnp.float32)
        ordering = jnp.argsort(owner_ids, stable=True)
        restore = jnp.argsort(ordering, stable=True)
        grouped = features(queries_here[ordering]).reshape(P_DEV, CONTS_PER, 2, HEADS, TAYLOR)
        numerator = jnp.einsum("pcthf,pfhv->pcthv", rounded(grouped), states, precision=highest)
        denominator = jnp.einsum("pcthf,pfh->pcth", grouped, norms, precision=highest)
        numerator = numerator.reshape(block_rows, 2, HEADS, HEAD_DIM)[restore]
        denominator = denominator.reshape(block_rows, 2, HEADS)[restore]
        tail_scores = jnp.einsum("cthf,chuf->cthu", queries_here, tail_k, precision=highest) * scale
        live_mask = (jnp.arange(TAIL)[None, :] < lengths[:, None]).astype(jnp.float32)
        tail_kernel = kernel_weight(tail_scores) * live_mask[:, None, None, :]
        new_scores = jnp.einsum("cthf,cjhf->cthj", queries_here, keys_here, precision=highest) * scale
        new_kernel = kernel_weight(new_scores) * causal[None, :, None, :]
        numerator = numerator + jnp.einsum("cthu,chuv->cthv", rounded(tail_kernel), tail_v, precision=highest)
        numerator = numerator + jnp.einsum("cthj,cjhv->cthv", rounded(new_kernel), values_here, precision=highest)
        denominator = denominator + jnp.sum(tail_kernel, axis=-1) + jnp.sum(new_kernel, axis=-1)
        return (numerator / denominator[..., None]).astype(jnp.bfloat16).reshape(block_rows, 2, D)

    heads_out = lax.map(one_block, jnp.arange(HOLDERS, dtype=jnp.int32)).reshape(CONT, 2, D).astype(jnp.float32)
    row_width = D // N_ROW
    result = token_values
    out_weights = w_out.astype(jnp.float32)
    for block_index in range(N_ROW):
        lower = block_index * row_width
        product = jnp.einsum("cte,ed->ctd", heads_out[:, :, lower:lower + row_width], out_weights[lower:lower + row_width], precision=highest)
        result = result + rounded(product)
    return result.astype(jnp.bfloat16)
```

```python
import functools

import jax
import jax.numpy as jnp
import numpy as np
from jax import lax
from jax.experimental import pallas as pl
from jax.experimental.pallas import tpu as pltpu
from jax.sharding import PartitionSpec as P

FEAT = 16
HEAD_DIM = 112
LANES = 128
TAYLOR_PAD = 384
F32 = jnp.float32
BF16 = jnp.bfloat16
VMEM_LIMIT = 48 * 1024 * 1024
CONTRACT_LAST = (((1,), (1,)), ((), ()))


def dot(a, b):
    return jnp.dot(a, b, preferred_element_type=F32)


def kappa(s):
    return 1.0 + s + 0.5 * s * s


def split3(x):
    hi = x.astype(BF16)
    rest = x - hi.astype(F32)
    mid = rest.astype(BF16)
    return hi, mid, (rest - mid.astype(F32)).astype(BF16)


def state_kernel(perm_ref, state_ref, norm_ref, out_ref):
    slots = out_ref.shape[1]
    taylor = state_ref.shape[1]
    width = 8 * slots
    perm = perm_ref[...]
    out_ref[0, :, :, taylor:] = jnp.zeros((slots, LANES, TAYLOR_PAD - taylor), BF16)
    for pair in range(HEAD_DIM // 16):
        parts = []
        for half in range(2):
            lower = (2 * pair + half) * width
            turned = lax.dot_general(
                perm, state_ref[0, :, lower : lower + width], CONTRACT_LAST, preferred_element_type=F32
            )
            parts.append(turned.reshape(slots, 8, taylor))
        both = jnp.concatenate(parts, axis=1).astype(BF16)
        out_ref[0, :, pair * 16 : pair * 16 + 16, :taylor] = both
    norm = norm_ref[0].astype(F32)
    wide = jnp.broadcast_to(norm[:, None, :], (slots, 16, taylor)).astype(BF16)
    out_ref[0, :, HEAD_DIM:, :taylor] = wide


def turn_states(cached_state, norm, heads, slots):
    taylor = cached_state.shape[1]
    width = 8 * slots
    perm = np.zeros((width, width), np.float32)
    for v in range(8):
        for q in range(slots):
            perm[q * 8 + v, v * slots + q] = 1
    return pl.pallas_call(
        state_kernel,
        grid=(heads,),
        in_specs=[
            pl.BlockSpec((width, width), lambda h: (0, 0)),
            pl.BlockSpec((1, taylor, HEAD_DIM * slots), lambda h: (0, 0, h)),
            pl.BlockSpec((1, slots, taylor), lambda h: (h, 0, 0)),
        ],
        out_specs=pl.BlockSpec((1, slots, LANES, TAYLOR_PAD), lambda h: (h, 0, 0, 0)),
        out_shape=jax.ShapeDtypeStruct((heads, slots, LANES, TAYLOR_PAD), BF16),
        compiler_params=pltpu.CompilerParams(vmem_limit_bytes=VMEM_LIMIT),
        cost_estimate=pl.CostEstimate(
            flops=20_000_000_000, bytes_accessed=45_000_000, transcendentals=0
        ),
    )(jnp.asarray(perm, BF16), cached_state, norm)


def prompt_kernel(q_ref, pick_ref, shift_ref, states_ref, out_ref, phi_ref):
    rows = q_ref.shape[0]
    slots = states_ref.shape[1]
    per = rows // slots
    width = q_ref.shape[1] // 2
    pick = pick_ref[0]
    for t in range(2):
        both = dot(q_ref[:, t * width : (t + 1) * width], pick)
        left = both[:, :TAYLOR_PAD] + shift_ref[0:1]
        right = both[:, TAYLOR_PAD:] + shift_ref[1:2]
        phi = left * right * shift_ref[2:3]
        hi = phi.astype(BF16)
        phi_ref[t] = hi
        phi_ref[2 + t] = (phi - hi.astype(F32)).astype(BF16)
    lane = lax.broadcasted_iota(jnp.int32, (2 * per, LANES), 1)
    for q in range(slots):
        pieces = [phi_ref[k, q * per : (q + 1) * per, :] for k in range(4)]
        got = lax.dot_general(
            jnp.concatenate(pieces, axis=0), states_ref[0, q], CONTRACT_LAST, preferred_element_type=F32
        )
        top = got[: 2 * per]
        den = top + got[2 * per :]
        hi, mid, low = split3(den)
        res = jnp.where(lane < HEAD_DIM, top, hi.astype(F32))
        res = jnp.where(lane == HEAD_DIM + 1, mid.astype(F32), res)
        res = jnp.where(lane == HEAD_DIM + 2, low.astype(F32), res).astype(BF16)
        out_ref[q * per : (q + 1) * per, :LANES] = res[:per]
        out_ref[q * per : (q + 1) * per, LANES:] = res[per:]


def pick_tables(heads):
    pick = np.zeros((heads, heads * FEAT, 2 * TAYLOR_PAD), np.float32)
    shift = np.zeros((8, TAYLOR_PAD), np.float32)
    shift[0, 0] = 1
    shift[1, : FEAT + 1] = 1
    shift[2, 0] = 1
    shift[2, 1 : FEAT + 1] = FEAT ** (-0.25)
    shift[2, FEAT + 1 : FEAT + 1 + FEAT * FEAT] = 0.5**0.5 / FEAT**0.5
    for h in range(heads):
        for a in range(FEAT):
            pick[h, h * FEAT + a, 1 + a] = 1
            for b in range(FEAT):
                f = 1 + FEAT + a * FEAT + b
                pick[h, h * FEAT + a, f] = 1
                pick[h, h * FEAT + b, TAYLOR_PAD + f] = 1
    return jnp.asarray(pick, BF16), jnp.asarray(shift, F32)


def prompt_terms(slot_queries, states, heads, slots):
    rows = slot_queries.shape[0]
    pick, shift = pick_tables(heads)
    return pl.pallas_call(
        prompt_kernel,
        grid=(heads,),
        in_specs=[
            pl.BlockSpec(slot_queries.shape, lambda h: (0, 0)),
            pl.BlockSpec((1,) + pick.shape[1:], lambda h: (h, 0, 0)),
            pl.BlockSpec(shift.shape, lambda h: (0, 0)),
            pl.BlockSpec((1, slots, LANES, TAYLOR_PAD), lambda h: (h, 0, 0, 0)),
        ],
        out_specs=pl.BlockSpec((rows, 2 * LANES), lambda h: (0, h)),
        out_shape=jax.ShapeDtypeStruct((rows, heads * 2 * LANES), BF16),
        scratch_shapes=[pltpu.VMEM((4, rows, TAYLOR_PAD), BF16)],
        compiler_params=pltpu.CompilerParams(vmem_limit_bytes=VMEM_LIMIT),
    )(slot_queries, pick, shift, states)


def tail_kernel(heads, tail, q_ref, tk_ref, tv_ref, len_ref, eq, rq, ew, rv, dw, rn, en, pad, out_ref):
    hf = heads * FEAT
    hd = heads * HEAD_DIM
    total = 2 * hf + hd
    block = q_ref.shape[0]
    lane = lax.broadcasted_iota(jnp.int32, (block, heads * tail), 1)
    live = lax.rem(lane, tail) < len_ref[...]
    keys = tk_ref[...].astype(F32)
    scale = FEAT ** (-0.5)
    new_k = [q_ref[:, t * total + hf : t * total + 2 * hf].astype(F32) for t in range(2)]
    new_v = [dot(q_ref[:, t * total + 2 * hf : (t + 1) * total], pad[...]) for t in range(2)]
    for t in range(2):
        query = q_ref[:, t * total : t * total + hf]
        spread = dot(query, eq[...])
        scores = dot((spread * keys).astype(BF16), rq[...]) * scale
        weight = jnp.where(live, kappa(scores), 0.0)
        hi = weight.astype(BF16)
        low = (weight - hi.astype(F32)).astype(BF16)
        acc = dot(hi, dw[...]) + dot(low, dw[...])
        for i in range(t + 1):
            product = (query.astype(F32) * new_k[i]).astype(BF16)
            fresh = kappa(dot(product, rn[...]) * scale)
            fresh_hi = fresh.astype(BF16)
            fresh_low = (fresh - fresh_hi.astype(F32)).astype(BF16)
            spread_hi = dot(fresh_hi, en[0])
            acc = acc + spread_hi * new_v[i] + dot(fresh_hi, en[1]) + dot(fresh_low, en[1])
        span = tail * HEAD_DIM
        for h in range(heads):
            wide = dot(hi, ew[:, h * span : (h + 1) * span])
            product = wide * tv_ref[:, h * span : (h + 1) * span].astype(F32)
            summed = dot(product.astype(BF16), rv[...])
            at = (2 * h + t) * LANES
            out_ref[:, at : at + LANES] = acc[:, h * LANES : (h + 1) * LANES] + summed


def tail_tables(heads, tail):
    hf, hd = heads * FEAT, heads * HEAD_DIM
    eq = np.zeros((hf, heads * tail * FEAT), np.float32)
    rq = np.zeros((heads * tail * FEAT, heads * tail), np.float32)
    ew = np.zeros((heads * tail, heads * tail * HEAD_DIM), np.float32)
    rv = np.zeros((tail * HEAD_DIM, LANES), np.float32)
    dw = np.zeros((heads * tail, heads * LANES), np.float32)
    rn = np.zeros((hf, LANES), np.float32)
    en = np.zeros((2, LANES, heads * LANES), np.float32)
    pad = np.zeros((hd, heads * LANES), np.float32)
    entries = np.arange(HEAD_DIM)
    for u in range(tail):
        rv[u * HEAD_DIM + entries, entries] = 1
    for h in range(heads):
        en[0, h, h * LANES + entries] = 1
        en[1, h, h * LANES + HEAD_DIM] = 1
        pad[h * HEAD_DIM + entries, h * LANES + entries] = 1
        rn[h * FEAT : (h + 1) * FEAT, h] = 1
        for u in range(tail):
            k = h * tail + u
            ew[k, k * HEAD_DIM + entries] = 1
            dw[k, h * LANES + HEAD_DIM] = 1
            for a in range(FEAT):
                eq[h * FEAT + a, k * FEAT + a] = 1
                rq[k * FEAT + a, k] = 1
    return [jnp.asarray(x, BF16) for x in (eq, rq, ew, rv, dw, rn, en, pad)]


def tail_terms(projected, tail_keys, tail_values, tail_length, heads, tail):
    conts = projected.shape[0]
    block = min(conts, 128)
    tables = tail_tables(heads, tail)

    def rows(array):
        return pl.BlockSpec((block, array.shape[1]), lambda i: (i, 0))

    def whole(array):
        return pl.BlockSpec(array.shape, lambda i, n=array.ndim: (0,) * n)

    return pl.pallas_call(
        functools.partial(tail_kernel, heads, tail),
        grid=(conts // block,),
        in_specs=[rows(projected), rows(tail_keys), rows(tail_values), rows(tail_length)]
        + [whole(x) for x in tables],
        out_specs=pl.BlockSpec((block, heads * 2 * LANES), lambda i: (i, 0)),
        out_shape=jax.ShapeDtypeStruct((conts, heads * 2 * LANES), F32),
        compiler_params=pltpu.CompilerParams(vmem_limit_bytes=VMEM_LIMIT),
        cost_estimate=pl.CostEstimate(
            flops=20_000_000_000, bytes_accessed=25_000_000, transcendentals=0
        ),
    )(projected, tail_keys, tail_values, tail_length, *tables)


def combine_kernel(heads, acc_ref, sent_at, kept_at, got_ref, kept_ref, pack, out_ref):
    block = acc_ref.shape[0]
    hd = heads * HEAD_DIM
    sent = sent_at[...] == lax.broadcasted_iota(jnp.int32, (block, got_ref.shape[0]), 1)
    kept = kept_at[...] == lax.broadcasted_iota(jnp.int32, (block, kept_ref.shape[0]), 1)
    sent = sent.astype(F32).astype(BF16)
    kept = kept.astype(F32).astype(BF16)
    prompt = dot(sent, got_ref[...]) + dot(kept, kept_ref[...])
    for t in range(2):
        parts = []
        for h in range(heads):
            at = (2 * h + t) * LANES
            terms = prompt[:, at : at + LANES]
            total = acc_ref[:, at : at + LANES] + terms
            den = total[:, HEAD_DIM : HEAD_DIM + 1]
            den = den + terms[:, HEAD_DIM + 1 : HEAD_DIM + 2] + terms[:, HEAD_DIM + 2 : HEAD_DIM + 3]
            parts.append((total / den).astype(BF16))
        wide = jnp.concatenate(parts, axis=1)
        out_ref[:, t * hd : (t + 1) * hd] = dot(wide, pack[...]).astype(BF16)


def combine(acc, sent_at, kept_at, got, kept, heads):
    conts = acc.shape[0]
    block = min(conts, 128)
    hd = heads * HEAD_DIM
    pack = np.zeros((heads * LANES, hd), np.float32)
    entries = np.arange(HEAD_DIM)
    for h in range(heads):
        pack[h * LANES + entries, h * HEAD_DIM + entries] = 1

    def rows(array):
        return pl.BlockSpec((block, array.shape[1]), lambda i: (i, 0))

    def whole(array):
        return pl.BlockSpec(array.shape, lambda i: (0, 0))

    pack = jnp.asarray(pack, BF16)
    return pl.pallas_call(
        functools.partial(combine_kernel, heads),
        grid=(conts // block,),
        in_specs=[rows(acc), rows(sent_at), rows(kept_at), whole(got), whole(kept), whole(pack)],
        out_specs=pl.BlockSpec((block, 2 * hd), lambda i: (i, 0)),
        out_shape=jax.ShapeDtypeStruct((conts, 2 * hd), BF16),
        compiler_params=pltpu.CompilerParams(vmem_limit_bytes=VMEM_LIMIT),
    )(acc, sent_at, kept_at, got, kept, pack)


def body(
    tokens,
    w_query,
    w_key,
    w_value,
    w_out,
    cached_state,
    cached_norm,
    slot_prompt,
    prompt_of,
    tail_keys,
    tail_values,
    tail_length,
):
    heads = w_query.shape[1] // FEAT
    depth = w_query.shape[0]
    hf, hd = heads * FEAT, heads * HEAD_DIM
    slots = slot_prompt.shape[0]
    conts = prompt_of.shape[0]
    per = conts // slots
    tail = tail_keys.shape[1] // hf
    axes = ("req", "col")
    holders = lax.axis_size(axes)
    capacity = (slots // 2 + holders - 2) // (holders - 1)
    me = lax.axis_index(axes)

    every = lax.all_gather(slot_prompt, axes, axis=0, tiled=True)
    flat = tokens.reshape(tokens.shape[0], 2 * depth)
    gathered = lax.all_gather(flat, "row", axis=0, tiled=True)
    value_weight = jnp.moveaxis(w_value.reshape(heads, depth, HEAD_DIM), 0, 1).reshape(depth, hd)
    stacked = jnp.concatenate([w_query, w_key, value_weight], axis=1)
    partial_sums = jnp.concatenate(
        [dot(gathered[:, t * depth : (t + 1) * depth], stacked).astype(BF16) for t in range(2)], axis=1
    )
    projected = lax.psum_scatter(partial_sums, "col", scatter_dimension=0, tiled=True)
    states = turn_states(cached_state, jnp.transpose(cached_norm, (2, 0, 1)), heads, slots)

    owner = (every // slots).reshape(holders, slots)
    before = jnp.arange(slots)[None, :] < jnp.arange(slots)[:, None]
    position = jnp.sum((owner[:, :, None] == owner[:, None, :]) & before[None], axis=2).reshape(-1)
    block_of = jnp.arange(holders * slots, dtype=jnp.int32) // slots * capacity + position
    local = prompt_of - me * slots
    found = prompt_of[:, None] == every[None, :]
    slot_at = jnp.max(jnp.where(found, jnp.arange(holders * slots, dtype=jnp.int32)[None, :], 0), axis=1)
    block_at = jnp.max(jnp.where(found, block_of[None, :], 0), axis=1)
    same = local[:, None] == local[None, :]
    rank = jnp.sum(same & (jnp.arange(conts)[None, :] < jnp.arange(conts)[:, None]), axis=1)
    away = slot_at // slots != me
    sent_at = jnp.where(away, block_at * per + rank, -1).astype(jnp.int32)
    kept_at = jnp.where(away, -1, slot_at % slots * per + rank).astype(jnp.int32)
    slot_owner = slot_prompt // slots
    mine_before = (slot_owner[:, None] == slot_owner[None, :]) & before
    slot_block = slot_owner * capacity + jnp.sum(mine_before, axis=1)
    slot_block = jnp.where(slot_owner == me, -1, slot_block)
    served = jnp.where(
        slot_block[:, None] < 0, -1, slot_block[:, None] * per + jnp.arange(per)[None, :]
    ).reshape(-1)
    sends = jnp.arange(holders * capacity * per)

    total = 2 * hf + hd
    queries = jnp.concatenate([projected[:, :hf], projected[:, total : total + hf]], axis=1)
    outgoing = dot((sends[:, None] == sent_at[None, :]).astype(BF16), queries).astype(BF16)
    incoming = lax.all_to_all(
        outgoing.reshape(holders, capacity * per, 2 * hf), axes, split_axis=0, concat_axis=0, tiled=True
    ).reshape(-1, 2 * hf)
    acc = tail_terms(projected, tail_keys, tail_values, tail_length[:, None], heads, tail)
    kept_queries = dot((jnp.arange(conts)[:, None] == kept_at[None, :]).astype(BF16), queries)
    slot_queries = dot((served[:, None] == sends[None, :]).astype(BF16), incoming) + kept_queries
    prompt = prompt_terms(slot_queries.astype(BF16), states, heads, slots)
    back = dot((sends[:, None] == served[None, :]).astype(BF16), prompt).astype(BF16)
    answers = lax.all_to_all(
        back.reshape(holders, capacity * per, -1), axes, split_axis=0, concat_axis=0, tiled=True
    ).reshape(back.shape)
    heads_out = combine(acc, sent_at[:, None], kept_at[:, None], answers, prompt, heads)

    everyone = lax.all_gather(heads_out, "col", axis=0, tiled=True)
    terms = jnp.concatenate(
        [dot(everyone[:, t * hd : (t + 1) * hd], w_out).astype(BF16) for t in range(2)], axis=1
    )
    mixed = lax.psum_scatter(terms, "row", scatter_dimension=0, tiled=True)
    return (mixed.astype(F32) + flat.astype(F32)).astype(BF16).reshape(tokens.shape)


def solution(mesh):
    return jax.shard_map(
        body,
        mesh=mesh,
        in_specs=(
            P(("req", "row"), None, "col"),
            P("col", "row"),
            P("col", "row"),
            P("row", "col"),
            P("row", "col"),
            P(("req", "col"), None, "row"),
            P(("req", "col"), None, "row"),
            P(("req", "col")),
            P(("req", "col")),
            P(("req", "col"), "row"),
            P(("req", "col"), "row"),
            P(("req", "col")),
        ),
        out_specs=P(("req", "row"), None, "col"),
        check_vma=False,
    )
```

```python
import functools

import jax
import jax.numpy as jnp
import numpy as np
from jax import lax
from jax.experimental import pallas as pl
from jax.experimental.pallas import tpu as pltpu
from jax.sharding import PartitionSpec as P

FEAT = 16
HEAD_DIM = 112
LANES = 128
TAYLOR_PAD = 384
F32 = jnp.float32
BF16 = jnp.bfloat16
VMEM_LIMIT = 48 * 1024 * 1024
CONTRACT_LAST = (((1,), (1,)), ((), ()))


def dot(a, b):
    return jnp.dot(a, b, preferred_element_type=F32)


def kappa(s):
    return 1.0 + s + 0.5 * s * s


def split3(x):
    hi = x.astype(BF16)
    rest = x - hi.astype(F32)
    mid = rest.astype(BF16)
    return hi, mid, (rest - mid.astype(F32)).astype(BF16)


def state_kernel(perm_ref, state_ref, norm_ref, out_ref):
    slots = out_ref.shape[1]
    taylor = state_ref.shape[1]
    width = 8 * slots
    perm = perm_ref[...]
    out_ref[0, :, :, taylor:] = jnp.zeros((slots, LANES, TAYLOR_PAD - taylor), BF16)
    for pair in range(HEAD_DIM // 16):
        parts = []
        for half in range(2):
            lower = (2 * pair + half) * width
            turned = lax.dot_general(
                perm, state_ref[0, :, lower : lower + width], CONTRACT_LAST, preferred_element_type=F32
            )
            parts.append(turned.reshape(slots, 8, taylor))
        both = jnp.concatenate(parts, axis=1).astype(BF16)
        out_ref[0, :, pair * 16 : pair * 16 + 16, :taylor] = both
    norm = norm_ref[0].astype(F32)
    wide = jnp.broadcast_to(norm[:, None, :], (slots, 16, taylor)).astype(BF16)
    out_ref[0, :, HEAD_DIM:, :taylor] = wide


def turn_states(cached_state, norm, heads, slots):
    taylor = cached_state.shape[1]
    width = 8 * slots
    perm = np.zeros((width, width), np.float32)
    for v in range(8):
        for q in range(slots):
            perm[q * 8 + v, v * slots + q] = 1
    return pl.pallas_call(
        state_kernel,
        grid=(heads,),
        in_specs=[
            pl.BlockSpec((width, width), lambda h: (0, 0)),
            pl.BlockSpec((1, taylor, HEAD_DIM * slots), lambda h: (0, 0, h)),
            pl.BlockSpec((1, slots, taylor), lambda h: (h, 0, 0)),
        ],
        out_specs=pl.BlockSpec((1, slots, LANES, TAYLOR_PAD), lambda h: (h, 0, 0, 0)),
        out_shape=jax.ShapeDtypeStruct((heads, slots, LANES, TAYLOR_PAD), BF16),
        compiler_params=pltpu.CompilerParams(vmem_limit_bytes=VMEM_LIMIT),
        cost_estimate=pl.CostEstimate(
            flops=20_000_000_000, bytes_accessed=45_000_000, transcendentals=0
        ),
    )(jnp.asarray(perm, BF16), cached_state, norm)


def prompt_kernel(q_ref, pick_ref, shift_ref, states_ref, out_ref, phi_ref):
    rows = q_ref.shape[0]
    slots = states_ref.shape[1]
    per = rows // slots
    width = q_ref.shape[1] // 2
    pick = pick_ref[0]
    for t in range(2):
        both = dot(q_ref[:, t * width : (t + 1) * width], pick)
        left = both[:, :TAYLOR_PAD] + shift_ref[0:1]
        right = both[:, TAYLOR_PAD:] + shift_ref[1:2]
        phi = left * right * shift_ref[2:3]
        hi = phi.astype(BF16)
        phi_ref[t] = hi
        phi_ref[2 + t] = (phi - hi.astype(F32)).astype(BF16)
    lane = lax.broadcasted_iota(jnp.int32, (2 * per, LANES), 1)
    for q in range(slots):
        pieces = [phi_ref[k, q * per : (q + 1) * per, :] for k in range(4)]
        got = lax.dot_general(
            jnp.concatenate(pieces, axis=0), states_ref[0, q], CONTRACT_LAST, preferred_element_type=F32
        )
        top = got[: 2 * per]
        den = top + got[2 * per :]
        hi, mid, low = split3(den)
        res = jnp.where(lane < HEAD_DIM, top, hi.astype(F32))
        res = jnp.where(lane == HEAD_DIM + 1, mid.astype(F32), res)
        res = jnp.where(lane == HEAD_DIM + 2, low.astype(F32), res).astype(BF16)
        out_ref[q * per : (q + 1) * per, :LANES] = res[:per]
        out_ref[q * per : (q + 1) * per, LANES:] = res[per:]


def pick_tables(heads):
    pick = np.zeros((heads, heads * FEAT, 2 * TAYLOR_PAD), np.float32)
    shift = np.zeros((8, TAYLOR_PAD), np.float32)
    shift[0, 0] = 1
    shift[1, : FEAT + 1] = 1
    shift[2, 0] = 1
    shift[2, 1 : FEAT + 1] = FEAT ** (-0.25)
    shift[2, FEAT + 1 : FEAT + 1 + FEAT * FEAT] = 0.5**0.5 / FEAT**0.5
    for h in range(heads):
        for a in range(FEAT):
            pick[h, h * FEAT + a, 1 + a] = 1
            for b in range(FEAT):
                f = 1 + FEAT + a * FEAT + b
                pick[h, h * FEAT + a, f] = 1
                pick[h, h * FEAT + b, TAYLOR_PAD + f] = 1
    return jnp.asarray(pick, BF16), jnp.asarray(shift, F32)


def prompt_terms(slot_queries, states, heads, slots):
    rows = slot_queries.shape[0]
    pick, shift = pick_tables(heads)
    return pl.pallas_call(
        prompt_kernel,
        grid=(heads,),
        in_specs=[
            pl.BlockSpec(slot_queries.shape, lambda h: (0, 0)),
            pl.BlockSpec((1,) + pick.shape[1:], lambda h: (h, 0, 0)),
            pl.BlockSpec(shift.shape, lambda h: (0, 0)),
            pl.BlockSpec((1, slots, LANES, TAYLOR_PAD), lambda h: (h, 0, 0, 0)),
        ],
        out_specs=pl.BlockSpec((rows, 2 * LANES), lambda h: (0, h)),
        out_shape=jax.ShapeDtypeStruct((rows, heads * 2 * LANES), BF16),
        scratch_shapes=[pltpu.VMEM((4, rows, TAYLOR_PAD), BF16)],
        compiler_params=pltpu.CompilerParams(vmem_limit_bytes=VMEM_LIMIT),
    )(slot_queries, pick, shift, states)


def tail_kernel(heads, tail, q_ref, tk_ref, tv_ref, len_ref, eq, rq, ew, rv, dw, rn, en, pad, out_ref):
    hf = heads * FEAT
    hd = heads * HEAD_DIM
    total = 2 * hf + hd
    block = q_ref.shape[0]
    lane = lax.broadcasted_iota(jnp.int32, (block, heads * tail), 1)
    live = lax.rem(lane, tail) < len_ref[...]
    keys = tk_ref[...].astype(F32)
    scale = FEAT ** (-0.5)
    new_k = [q_ref[:, t * total + hf : t * total + 2 * hf].astype(F32) for t in range(2)]
    new_v = [dot(q_ref[:, t * total + 2 * hf : (t + 1) * total], pad[...]) for t in range(2)]
    for t in range(2):
        query = q_ref[:, t * total : t * total + hf]
        spread = dot(query, eq[...])
        scores = dot((spread * keys).astype(BF16), rq[...]) * scale
        weight = jnp.where(live, kappa(scores), 0.0)
        hi = weight.astype(BF16)
        low = (weight - hi.astype(F32)).astype(BF16)
        acc = dot(hi, dw[...]) + dot(low, dw[...])
        for i in range(t + 1):
            product = (query.astype(F32) * new_k[i]).astype(BF16)
            fresh = kappa(dot(product, rn[...]) * scale)
            fresh_hi = fresh.astype(BF16)
            fresh_low = (fresh - fresh_hi.astype(F32)).astype(BF16)
            spread_hi = dot(fresh_hi, en[0])
            acc = acc + spread_hi * new_v[i] + dot(fresh_hi, en[1]) + dot(fresh_low, en[1])
        span = tail * HEAD_DIM
        for h in range(heads):
            wide = dot(hi, ew[:, h * span : (h + 1) * span])
            product = wide * tv_ref[:, h * span : (h + 1) * span].astype(F32)
            summed = dot(product.astype(BF16), rv[...])
            at = (2 * h + t) * LANES
            out_ref[:, at : at + LANES] = acc[:, h * LANES : (h + 1) * LANES] + summed


def tail_tables(heads, tail):
    hf, hd = heads * FEAT, heads * HEAD_DIM
    eq = np.zeros((hf, heads * tail * FEAT), np.float32)
    rq = np.zeros((heads * tail * FEAT, heads * tail), np.float32)
    ew = np.zeros((heads * tail, heads * tail * HEAD_DIM), np.float32)
    rv = np.zeros((tail * HEAD_DIM, LANES), np.float32)
    dw = np.zeros((heads * tail, heads * LANES), np.float32)
    rn = np.zeros((hf, LANES), np.float32)
    en = np.zeros((2, LANES, heads * LANES), np.float32)
    pad = np.zeros((hd, heads * LANES), np.float32)
    entries = np.arange(HEAD_DIM)
    for u in range(tail):
        rv[u * HEAD_DIM + entries, entries] = 1
    for h in range(heads):
        en[0, h, h * LANES + entries] = 1
        en[1, h, h * LANES + HEAD_DIM] = 1
        pad[h * HEAD_DIM + entries, h * LANES + entries] = 1
        rn[h * FEAT : (h + 1) * FEAT, h] = 1
        for u in range(tail):
            k = h * tail + u
            ew[k, k * HEAD_DIM + entries] = 1
            dw[k, h * LANES + HEAD_DIM] = 1
            for a in range(FEAT):
                eq[h * FEAT + a, k * FEAT + a] = 1
                rq[k * FEAT + a, k] = 1
    return [jnp.asarray(x, BF16) for x in (eq, rq, ew, rv, dw, rn, en, pad)]


def tail_terms(projected, tail_keys, tail_values, tail_length, heads, tail):
    conts = projected.shape[0]
    block = min(conts, 128)
    tables = tail_tables(heads, tail)

    def rows(array):
        return pl.BlockSpec((block, array.shape[1]), lambda i: (i, 0))

    def whole(array):
        return pl.BlockSpec(array.shape, lambda i, n=array.ndim: (0,) * n)

    return pl.pallas_call(
        functools.partial(tail_kernel, heads, tail),
        grid=(conts // block,),
        in_specs=[rows(projected), rows(tail_keys), rows(tail_values), rows(tail_length)]
        + [whole(x) for x in tables],
        out_specs=pl.BlockSpec((block, heads * 2 * LANES), lambda i: (i, 0)),
        out_shape=jax.ShapeDtypeStruct((conts, heads * 2 * LANES), F32),
        compiler_params=pltpu.CompilerParams(vmem_limit_bytes=VMEM_LIMIT),
        cost_estimate=pl.CostEstimate(
            flops=20_000_000_000, bytes_accessed=25_000_000, transcendentals=0
        ),
    )(projected, tail_keys, tail_values, tail_length, *tables)


def combine_kernel(heads, acc_ref, sent_at, kept_at, got_ref, kept_ref, pack, out_ref):
    block = acc_ref.shape[0]
    hd = heads * HEAD_DIM
    sent = sent_at[...] == lax.broadcasted_iota(jnp.int32, (block, got_ref.shape[0]), 1)
    kept = kept_at[...] == lax.broadcasted_iota(jnp.int32, (block, kept_ref.shape[0]), 1)
    sent = sent.astype(F32).astype(BF16)
    kept = kept.astype(F32).astype(BF16)
    prompt = dot(sent, got_ref[...]) + dot(kept, kept_ref[...])
    for t in range(2):
        parts = []
        for h in range(heads):
            at = (2 * h + t) * LANES
            terms = prompt[:, at : at + LANES]
            total = acc_ref[:, at : at + LANES] + terms
            den = total[:, HEAD_DIM : HEAD_DIM + 1]
            den = den + terms[:, HEAD_DIM + 1 : HEAD_DIM + 2] + terms[:, HEAD_DIM + 2 : HEAD_DIM + 3]
            parts.append((total / den).astype(BF16))
        wide = jnp.concatenate(parts, axis=1)
        out_ref[:, t * hd : (t + 1) * hd] = dot(wide, pack[...]).astype(BF16)


def combine(acc, sent_at, kept_at, got, kept, heads):
    conts = acc.shape[0]
    block = min(conts, 128)
    hd = heads * HEAD_DIM
    pack = np.zeros((heads * LANES, hd), np.float32)
    entries = np.arange(HEAD_DIM)
    for h in range(heads):
        pack[h * LANES + entries, h * HEAD_DIM + entries] = 1

    def rows(array):
        return pl.BlockSpec((block, array.shape[1]), lambda i: (i, 0))

    def whole(array):
        return pl.BlockSpec(array.shape, lambda i: (0, 0))

    pack = jnp.asarray(pack, BF16)
    return pl.pallas_call(
        functools.partial(combine_kernel, heads),
        grid=(conts // block,),
        in_specs=[rows(acc), rows(sent_at), rows(kept_at), whole(got), whole(kept), whole(pack)],
        out_specs=pl.BlockSpec((block, 2 * hd), lambda i: (i, 0)),
        out_shape=jax.ShapeDtypeStruct((conts, 2 * hd), BF16),
        compiler_params=pltpu.CompilerParams(vmem_limit_bytes=VMEM_LIMIT),
    )(acc, sent_at, kept_at, got, kept, pack)


def remote(src, dst, send, recv, **target):
    return pltpu.make_async_remote_copy(
        src_ref=src,
        dst_ref=dst,
        send_sem=send,
        recv_sem=recv,
        device_id=target,
        device_id_type=pl.DeviceIdType.MESH,
    )


def greet(targets):
    barrier = pltpu.get_barrier_semaphore()
    for target in targets:
        pl.semaphore_signal(barrier, inc=1, device_id=target, device_id_type=pl.DeviceIdType.MESH)
    pl.semaphore_wait(barrier, len(targets))


def places():
    row, col = lax.axis_index("row"), lax.axis_index("col")
    across = lax.rem(col + 2, 4)
    core = lax.rem(col, 2)
    sibling = col + 1 - 2 * core
    return row, 1 - row, col, across, core, sibling


def front_kernel(
    x, w, wo, tok, wall, woall, via, y_send, y_recv, c_send, c_recv, w_send, w_recv, o_send, o_recv, l_sem
):
    row, partner, col, across, core, sibling = places()
    greet([{"row": partner}] + [{"col": lax.rem(col + k, 4)} for k in (1, 2, 3)])
    size = tok.shape[1] // 2

    def to_row(j):
        rows = pl.ds(j * size, size)
        return remote(x.at[rows], via.at[rows], y_send.at[j], y_recv.at[j], row=partner)

    def holder_of(source, j):
        return 2 * (row if source == 0 else partner) + j // 2

    def ends(source, j):
        src = (x if source == 0 else via).at[pl.ds(j * size, size)]
        return src, tok.at[col, pl.ds((j % 2) * size, size)], c_recv.at[col, j % 2]

    def to_holder(source, j):
        src, dst, arrival = ends(source, j)
        return remote(src, dst, c_send.at[source * 4 + j], arrival, col=holder_of(source, j))

    def start_holder(source, j):
        @pl.when(holder_of(source, j) != col)
        def _():
            to_holder(source, j).start()

        @pl.when(holder_of(source, j) == col)
        def _():
            pltpu.make_async_copy(*ends(source, j)).start()

    for j in range(4):
        to_row(j).start()
    w_across = remote(w, wall.at[col], w_send.at[0], w_recv.at[0], col=across)
    w_side = remote(w, wall.at[col], w_send.at[1], w_recv.at[1], col=sibling)
    w_here = pltpu.make_async_copy(w, wall.at[col], l_sem.at[0])
    o_there = remote(wo, woall.at[row], o_send, o_recv, row=partner)
    o_here = pltpu.make_async_copy(wo, woall.at[row], l_sem.at[1])
    for j in range(4):
        start_holder(0, j)
    w_across.start()
    w_side.start()
    w_here.start()
    o_here.start()
    for j in range(4):
        to_row(j).wait_recv()
        start_holder(1, j)
    o_there.start()
    w_across.wait_recv()
    w_on = remote(wall.at[across], wall.at[across], w_send.at[2], w_recv.at[2], col=sibling)
    w_on.start()
    for source in range(2):
        for j in range(4):

            @pl.when(holder_of(source, j) != col)
            def _():
                to_holder(source, j).wait_send()

    for k in range(4):
        for part in range(2):
            rows = pl.ds(part * size, size)

            @pl.when(col != k)
            def _():
                remote(
                    tok.at[k, rows], tok.at[k, rows], c_send.at[0], c_recv.at[k, part], col=across
                ).wait_recv()

            @pl.when(col == k)
            def _():
                pltpu.make_async_copy(tok.at[k, rows], tok.at[k, rows], c_recv.at[k, part]).wait()

    for j in range(4):
        to_row(j).wait_send()
    w_across.wait_send()
    w_side.wait()
    w_on.wait()
    w_here.wait()
    o_there.wait()
    o_here.wait()


def front(x, w, wo, conts):
    dma = pltpu.SemaphoreType.DMA
    return pl.pallas_call(
        front_kernel,
        in_specs=[pl.BlockSpec(memory_space=pl.ANY)] * 3,
        out_specs=[pl.BlockSpec(memory_space=pl.ANY)] * 4,
        out_shape=[
            jax.ShapeDtypeStruct((4, conts, x.shape[1]), BF16),
            jax.ShapeDtypeStruct((4,) + w.shape, BF16),
            jax.ShapeDtypeStruct((2,) + wo.shape, BF16),
            jax.ShapeDtypeStruct(x.shape, BF16),
        ],
        scratch_shapes=[
            dma((4,)), dma((4,)), dma((8,)), dma((4, 2)), dma((3,)), dma((3,)), dma, dma, dma((2,)),
        ],
        compiler_params=pltpu.CompilerParams(collective_id=0, has_side_effects=True),
    )(x, w, wo)


def back_kernel(h, hall, via, sx, rx, sy, ry, ss, rs, sf, rf, sl):
    row, partner, col, across, core, sibling = places()
    greet([{"row": partner}, {"col": across}, {"col": sibling}])
    pieces = 4
    size = h.shape[0] // pieces
    stays = col // 2 == row

    def at(ref, j):
        return ref.at[pl.ds(j * size, size)]

    def slot(b, half, j):
        return hall.at[b, half, pl.ds(j * size, size)]

    def x_via(j):
        return remote(at(h, j), at(via, j), sx.at[j], rx.at[j], col=across)

    def x_final(j):
        return remote(at(h, j), slot(core, row, j), sx.at[j], rx.at[j], col=across)

    def y_own(j):
        return remote(at(h, j), slot(core, row, j), sy.at[j], ry.at[j], row=partner)

    def y_via(j):
        return remote(at(via, j), slot(core, row, j), sy.at[j], ry.at[j], row=partner)

    def side_own(j):
        return remote(at(h, j), slot(core, row, j), ss.at[j], rs.at[j], col=sibling)

    def side_got(j):
        return remote(slot(core, row, j), slot(core, row, j), ss.at[j], rs.at[j], col=sibling)

    def side_far(j):
        return remote(slot(core, partner, j), slot(core, partner, j), sf.at[j], rf.at[j], col=sibling)

    def keep(j):
        return pltpu.make_async_copy(at(h, j), slot(core, row, j), sl.at[j])

    for j in range(pieces):

        @pl.when(stays)
        def _():
            x_final(j).start()
            side_own(j).start()
            keep(j).start()

        @pl.when(jnp.logical_not(stays))
        def _():
            x_via(j).start()
            y_own(j).start()

    for j in range(pieces):

        @pl.when(stays)
        def _():
            x_via(j).wait_recv()
            y_via(j).start()

        @pl.when(jnp.logical_not(stays))
        def _():
            remote(slot(core, row, j), slot(core, row, j), sx.at[j], rx.at[j], col=across).wait_recv()
            side_got(j).start()

    for j in range(pieces):
        remote(slot(core, partner, j), slot(core, partner, j), sy.at[j], ry.at[j], row=partner).wait_recv()
        side_far(j).start()
    for j in range(pieces):
        near = slot(1 - core, row, j)
        far = slot(1 - core, partner, j)
        remote(near, near, ss.at[j], rs.at[j], col=sibling).wait_recv()
        remote(far, far, sf.at[j], rf.at[j], col=sibling).wait_recv()
        side_far(j).wait_send()

        @pl.when(stays)
        def _():
            x_final(j).wait_send()
            y_via(j).wait_send()
            side_own(j).wait_send()
            keep(j).wait()

        @pl.when(jnp.logical_not(stays))
        def _():
            x_via(j).wait_send()
            y_own(j).wait_send()
            side_got(j).wait_send()


def back(h):
    dma = pltpu.SemaphoreType.DMA((4,))
    return pl.pallas_call(
        back_kernel,
        in_specs=[pl.BlockSpec(memory_space=pl.ANY)],
        out_specs=[pl.BlockSpec(memory_space=pl.ANY)] * 2,
        out_shape=[
            jax.ShapeDtypeStruct((2, 2) + h.shape, BF16),
            jax.ShapeDtypeStruct(h.shape, BF16),
        ],
        scratch_shapes=[dma] * 9,
        compiler_params=pltpu.CompilerParams(collective_id=1, has_side_effects=True),
    )(h)[0]


def project_kernel(tok_ref, w_ref, out_ref):
    depth, total = w_ref.shape[1:]
    for t in range(2):
        acc = jnp.zeros((tok_ref.shape[1], total), F32)
        for k in range(w_ref.shape[0]):
            acc = acc + dot(tok_ref[k, :, t * depth : (t + 1) * depth], w_ref[k])
        out_ref[:, t * total : (t + 1) * total] = acc.astype(BF16)


def project(tok, w):
    conts, total = tok.shape[1], w.shape[2]
    block = 128
    return pl.pallas_call(
        project_kernel,
        grid=(conts // block,),
        in_specs=[
            pl.BlockSpec((tok.shape[0], block, tok.shape[2]), lambda i: (0, i, 0)),
            pl.BlockSpec(w.shape, lambda i: (0, 0, 0)),
        ],
        out_specs=pl.BlockSpec((block, 2 * total), lambda i: (i, 0)),
        out_shape=jax.ShapeDtypeStruct((conts, 2 * total), BF16),
        compiler_params=pltpu.CompilerParams(vmem_limit_bytes=VMEM_LIMIT),
    )(tok, w)


def output_kernel(h_ref, w_ref, x_ref, out_ref):
    hd, depth = w_ref.shape[1:]
    for t in range(2):
        acc = x_ref[:, t * depth : (t + 1) * depth].astype(F32)
        for half in range(2):
            part = dot(h_ref[0, half, :, t * hd : (t + 1) * hd], w_ref[half])
            acc = acc + part.astype(BF16).astype(F32)
        out_ref[:, t * depth : (t + 1) * depth] = acc.astype(BF16)


def output(hall, w, flat):
    block = 128
    steps = hall.shape[2] // block
    return pl.pallas_call(
        output_kernel,
        grid=(2, steps),
        in_specs=[
            pl.BlockSpec((1, 2, block, hall.shape[3]), lambda b, i: (b, 0, i, 0)),
            pl.BlockSpec(w.shape, lambda b, i: (0, 0, 0)),
            pl.BlockSpec((block, flat.shape[1]), lambda b, i: (b * steps + i, 0)),
        ],
        out_specs=pl.BlockSpec((block, flat.shape[1]), lambda b, i: (b * steps + i, 0)),
        out_shape=jax.ShapeDtypeStruct(flat.shape, BF16),
        compiler_params=pltpu.CompilerParams(vmem_limit_bytes=VMEM_LIMIT),
    )(hall, w, flat)


def body(
    tokens,
    w_query,
    w_key,
    w_value,
    w_out,
    cached_state,
    cached_norm,
    slot_prompt,
    prompt_of,
    tail_keys,
    tail_values,
    tail_length,
):
    heads = w_query.shape[1] // FEAT
    depth = w_query.shape[0]
    hf, hd = heads * FEAT, heads * HEAD_DIM
    slots = slot_prompt.shape[0]
    conts = prompt_of.shape[0]
    per = conts // slots
    tail = tail_keys.shape[1] // hf
    axes = ("req", "col")
    holders = lax.axis_size(axes)
    capacity = (slots // 2 + holders - 2) // (holders - 1)
    me = lax.axis_index(axes)

    pair = jnp.stack([slot_prompt // slots, slot_prompt % slots]).astype(BF16)
    pair = jnp.zeros((16, LANES), BF16).at[:2, :slots].set(pair)
    pairs = lax.all_gather(pair, axes, axis=0, tiled=True).reshape(holders, 16, LANES)[:, :2, :slots]
    pairs = pairs.astype(jnp.int32)
    every = (pairs[:, 0] * slots + pairs[:, 1]).reshape(-1)
    flat = tokens.reshape(tokens.shape[0], 2 * depth)
    value_weight = jnp.moveaxis(w_value.reshape(heads, depth, HEAD_DIM), 0, 1).reshape(depth, hd)
    stacked = jnp.concatenate([w_query, w_key, value_weight], axis=1)
    direct = lax.axis_size("row") == 2 and lax.axis_size("col") == 4
    if direct:
        tok, w_all, wo_all, _ = front(flat, stacked, w_out, conts)
        projected = project(tok, w_all)
    else:
        gathered = lax.all_gather(flat, "row", axis=0, tiled=True)
        partial_sums = [
            dot(gathered[:, t * depth : (t + 1) * depth], stacked).astype(BF16) for t in range(2)
        ]
        projected = lax.psum_scatter(
            jnp.concatenate(partial_sums, axis=1), "col", scatter_dimension=0, tiled=True
        )
    states = turn_states(cached_state, jnp.transpose(cached_norm, (2, 0, 1)), heads, slots)

    owner = (every // slots).reshape(holders, slots)
    before = jnp.arange(slots)[None, :] < jnp.arange(slots)[:, None]
    position = jnp.sum((owner[:, :, None] == owner[:, None, :]) & before[None], axis=2).reshape(-1)
    block_of = jnp.arange(holders * slots, dtype=jnp.int32) // slots * capacity + position
    local = prompt_of - me * slots
    found = prompt_of[:, None] == every[None, :]
    slot_at = jnp.max(jnp.where(found, jnp.arange(holders * slots, dtype=jnp.int32)[None, :], 0), axis=1)
    block_at = jnp.max(jnp.where(found, block_of[None, :], 0), axis=1)
    same = local[:, None] == local[None, :]
    rank = jnp.sum(same & (jnp.arange(conts)[None, :] < jnp.arange(conts)[:, None]), axis=1)
    away = slot_at // slots != me
    sent_at = jnp.where(away, block_at * per + rank, -1).astype(jnp.int32)
    kept_at = jnp.where(away, -1, slot_at % slots * per + rank).astype(jnp.int32)
    slot_owner = slot_prompt // slots
    mine_before = (slot_owner[:, None] == slot_owner[None, :]) & before
    slot_block = slot_owner * capacity + jnp.sum(mine_before, axis=1)
    slot_block = jnp.where(slot_owner == me, -1, slot_block)
    served = jnp.where(
        slot_block[:, None] < 0, -1, slot_block[:, None] * per + jnp.arange(per)[None, :]
    ).reshape(-1)
    sends = jnp.arange(holders * capacity * per)

    total = 2 * hf + hd
    queries = jnp.concatenate([projected[:, :hf], projected[:, total : total + hf]], axis=1)
    outgoing = dot((sends[:, None] == sent_at[None, :]).astype(BF16), queries).astype(BF16)
    incoming = lax.all_to_all(
        outgoing.reshape(holders, capacity * per, 2 * hf), axes, split_axis=0, concat_axis=0, tiled=True
    ).reshape(-1, 2 * hf)
    acc = tail_terms(projected, tail_keys, tail_values, tail_length[:, None], heads, tail)
    kept_queries = dot((jnp.arange(conts)[:, None] == kept_at[None, :]).astype(BF16), queries)
    slot_queries = dot((served[:, None] == sends[None, :]).astype(BF16), incoming) + kept_queries
    prompt = prompt_terms(slot_queries.astype(BF16), states, heads, slots)
    replies = dot((sends[:, None] == served[None, :]).astype(BF16), prompt).astype(BF16)
    answers = lax.all_to_all(
        replies.reshape(holders, capacity * per, -1), axes, split_axis=0, concat_axis=0, tiled=True
    ).reshape(replies.shape)
    heads_out = combine(acc, sent_at[:, None], kept_at[:, None], answers, prompt, heads)

    if direct:
        return output(back(heads_out), wo_all, flat).reshape(tokens.shape)
    everyone = lax.all_gather(heads_out, "col", axis=0, tiled=True)
    terms = jnp.concatenate(
        [dot(everyone[:, t * hd : (t + 1) * hd], w_out).astype(BF16) for t in range(2)], axis=1
    )
    mixed = lax.psum_scatter(terms, "row", scatter_dimension=0, tiled=True)
    return (mixed.astype(F32) + flat.astype(F32)).astype(BF16).reshape(tokens.shape)


def solution(mesh):
    return jax.shard_map(
        body,
        mesh=mesh,
        in_specs=(
            P(("req", "row"), None, "col"),
            P("col", "row"),
            P("col", "row"),
            P("row", "col"),
            P("row", "col"),
            P(("req", "col"), None, "row"),
            P(("req", "col"), None, "row"),
            P(("req", "col")),
            P(("req", "col")),
            P(("req", "col"), "row"),
            P(("req", "col"), "row"),
            P(("req", "col")),
        ),
        out_specs=P(("req", "row"), None, "col"),
        check_vma=False,
    )
```

```python
import functools

import jax
import jax.numpy as jnp
import numpy as np
from jax import lax
from jax.experimental import pallas as pl
from jax.experimental.pallas import tpu as pltpu
from jax.sharding import PartitionSpec as P

FEAT = 16
HEAD_DIM = 112
LANES = 128
TAYLOR_PAD = 384
F32 = jnp.float32
BF16 = jnp.bfloat16
VMEM_LIMIT = 48 * 1024 * 1024
CONTRACT_LAST = (((1,), (1,)), ((), ()))


def dot(a, b):
    return jnp.dot(a, b, preferred_element_type=F32)


def kappa(s):
    return 1.0 + s + 0.5 * s * s


def split3(x):
    hi = x.astype(BF16)
    rest = x - hi.astype(F32)
    mid = rest.astype(BF16)
    return hi, mid, (rest - mid.astype(F32)).astype(BF16)


def state_kernel(perm_ref, state_ref, norm_ref, out_ref):
    slots = out_ref.shape[1]
    taylor = state_ref.shape[1]
    width = 8 * slots
    perm = perm_ref[...]
    out_ref[0, :, :, taylor:] = jnp.zeros((slots, LANES, TAYLOR_PAD - taylor), BF16)
    for pair in range(HEAD_DIM // 16):
        parts = []
        for half in range(2):
            lower = (2 * pair + half) * width
            turned = lax.dot_general(
                perm, state_ref[0, :, lower : lower + width], CONTRACT_LAST, preferred_element_type=F32
            )
            parts.append(turned.reshape(slots, 8, taylor))
        both = jnp.concatenate(parts, axis=1).astype(BF16)
        out_ref[0, :, pair * 16 : pair * 16 + 16, :taylor] = both
    norm = norm_ref[0].astype(F32)
    wide = jnp.broadcast_to(norm[:, None, :], (slots, 16, taylor)).astype(BF16)
    out_ref[0, :, HEAD_DIM:, :taylor] = wide


def turn_states(cached_state, norm, heads, slots):
    taylor = cached_state.shape[1]
    width = 8 * slots
    perm = np.zeros((width, width), np.float32)
    for v in range(8):
        for q in range(slots):
            perm[q * 8 + v, v * slots + q] = 1
    return pl.pallas_call(
        state_kernel,
        grid=(heads,),
        in_specs=[
            pl.BlockSpec((width, width), lambda h: (0, 0)),
            pl.BlockSpec((1, taylor, HEAD_DIM * slots), lambda h: (0, 0, h)),
            pl.BlockSpec((1, slots, taylor), lambda h: (h, 0, 0)),
        ],
        out_specs=pl.BlockSpec((1, slots, LANES, TAYLOR_PAD), lambda h: (h, 0, 0, 0)),
        out_shape=jax.ShapeDtypeStruct((heads, slots, LANES, TAYLOR_PAD), BF16),
        compiler_params=pltpu.CompilerParams(vmem_limit_bytes=VMEM_LIMIT),
        cost_estimate=pl.CostEstimate(
            flops=20_000_000_000, bytes_accessed=45_000_000, transcendentals=0
        ),
    )(jnp.asarray(perm, BF16), cached_state, norm)


def prompt_kernel(q_ref, pick_ref, shift_ref, states_ref, out_ref, phi_ref):
    rows = q_ref.shape[0]
    slots = states_ref.shape[1]
    per = rows // slots
    width = q_ref.shape[1] // 2
    pick = pick_ref[0]
    for t in range(2):
        both = dot(q_ref[:, t * width : (t + 1) * width], pick)
        left = both[:, :TAYLOR_PAD] + shift_ref[0:1]
        right = both[:, TAYLOR_PAD:] + shift_ref[1:2]
        phi = left * right * shift_ref[2:3]
        hi = phi.astype(BF16)
        phi_ref[t] = hi
        phi_ref[2 + t] = (phi - hi.astype(F32)).astype(BF16)
    lane = lax.broadcasted_iota(jnp.int32, (2 * per, LANES), 1)
    for q in range(slots):
        pieces = [phi_ref[k, q * per : (q + 1) * per, :] for k in range(4)]
        got = lax.dot_general(
            jnp.concatenate(pieces, axis=0), states_ref[0, q], CONTRACT_LAST, preferred_element_type=F32
        )
        top = got[: 2 * per]
        den = top + got[2 * per :]
        hi, mid, low = split3(den)
        res = jnp.where(lane < HEAD_DIM, top, hi.astype(F32))
        res = jnp.where(lane == HEAD_DIM + 1, mid.astype(F32), res)
        res = jnp.where(lane == HEAD_DIM + 2, low.astype(F32), res).astype(BF16)
        out_ref[q * per : (q + 1) * per, :LANES] = res[:per]
        out_ref[q * per : (q + 1) * per, LANES:] = res[per:]


def pick_tables(heads):
    pick = np.zeros((heads, heads * FEAT, 2 * TAYLOR_PAD), np.float32)
    shift = np.zeros((8, TAYLOR_PAD), np.float32)
    shift[0, 0] = 1
    shift[1, : FEAT + 1] = 1
    shift[2, 0] = 1
    shift[2, 1 : FEAT + 1] = FEAT ** (-0.25)
    shift[2, FEAT + 1 : FEAT + 1 + FEAT * FEAT] = 0.5**0.5 / FEAT**0.5
    for h in range(heads):
        for a in range(FEAT):
            pick[h, h * FEAT + a, 1 + a] = 1
            for b in range(FEAT):
                f = 1 + FEAT + a * FEAT + b
                pick[h, h * FEAT + a, f] = 1
                pick[h, h * FEAT + b, TAYLOR_PAD + f] = 1
    return jnp.asarray(pick, BF16), jnp.asarray(shift, F32)


def prompt_terms(slot_queries, states, heads, slots):
    rows = slot_queries.shape[0]
    pick, shift = pick_tables(heads)
    return pl.pallas_call(
        prompt_kernel,
        grid=(heads,),
        in_specs=[
            pl.BlockSpec(slot_queries.shape, lambda h: (0, 0)),
            pl.BlockSpec((1,) + pick.shape[1:], lambda h: (h, 0, 0)),
            pl.BlockSpec(shift.shape, lambda h: (0, 0)),
            pl.BlockSpec((1, slots, LANES, TAYLOR_PAD), lambda h: (h, 0, 0, 0)),
        ],
        out_specs=pl.BlockSpec((rows, 2 * LANES), lambda h: (0, h)),
        out_shape=jax.ShapeDtypeStruct((rows, heads * 2 * LANES), BF16),
        scratch_shapes=[pltpu.VMEM((4, rows, TAYLOR_PAD), BF16)],
        compiler_params=pltpu.CompilerParams(vmem_limit_bytes=VMEM_LIMIT),
    )(slot_queries, pick, shift, states)


def tail_kernel(heads, tail, q_ref, tk_ref, tv_ref, len_ref, eq, rq, ew, rv, dw, rn, en, pad, out_ref):
    hf = heads * FEAT
    hd = heads * HEAD_DIM
    total = 2 * hf + hd
    block = q_ref.shape[0]
    lane = lax.broadcasted_iota(jnp.int32, (block, heads * tail), 1)
    live = lax.rem(lane, tail) < len_ref[...]
    keys = tk_ref[...].astype(F32)
    scale = FEAT ** (-0.5)
    new_k = [q_ref[:, t * total + hf : t * total + 2 * hf].astype(F32) for t in range(2)]
    new_v = [dot(q_ref[:, t * total + 2 * hf : (t + 1) * total], pad[...]) for t in range(2)]
    for t in range(2):
        query = q_ref[:, t * total : t * total + hf]
        spread = dot(query, eq[...])
        scores = dot((spread * keys).astype(BF16), rq[...]) * scale
        weight = jnp.where(live, kappa(scores), 0.0)
        hi = weight.astype(BF16)
        low = (weight - hi.astype(F32)).astype(BF16)
        acc = dot(hi, dw[...]) + dot(low, dw[...])
        for i in range(t + 1):
            product = (query.astype(F32) * new_k[i]).astype(BF16)
            fresh = kappa(dot(product, rn[...]) * scale)
            fresh_hi = fresh.astype(BF16)
            fresh_low = (fresh - fresh_hi.astype(F32)).astype(BF16)
            spread_hi = dot(fresh_hi, en[0])
            acc = acc + spread_hi * new_v[i] + dot(fresh_hi, en[1]) + dot(fresh_low, en[1])
        span = tail * HEAD_DIM
        for h in range(heads):
            wide = dot(hi, ew[:, h * span : (h + 1) * span])
            product = wide * tv_ref[:, h * span : (h + 1) * span].astype(F32)
            summed = dot(product.astype(BF16), rv[...])
            at = (2 * h + t) * LANES
            out_ref[:, at : at + LANES] = acc[:, h * LANES : (h + 1) * LANES] + summed


def tail_tables(heads, tail):
    hf, hd = heads * FEAT, heads * HEAD_DIM
    eq = np.zeros((hf, heads * tail * FEAT), np.float32)
    rq = np.zeros((heads * tail * FEAT, heads * tail), np.float32)
    ew = np.zeros((heads * tail, heads * tail * HEAD_DIM), np.float32)
    rv = np.zeros((tail * HEAD_DIM, LANES), np.float32)
    dw = np.zeros((heads * tail, heads * LANES), np.float32)
    rn = np.zeros((hf, LANES), np.float32)
    en = np.zeros((2, LANES, heads * LANES), np.float32)
    pad = np.zeros((hd, heads * LANES), np.float32)
    entries = np.arange(HEAD_DIM)
    for u in range(tail):
        rv[u * HEAD_DIM + entries, entries] = 1
    for h in range(heads):
        en[0, h, h * LANES + entries] = 1
        en[1, h, h * LANES + HEAD_DIM] = 1
        pad[h * HEAD_DIM + entries, h * LANES + entries] = 1
        rn[h * FEAT : (h + 1) * FEAT, h] = 1
        for u in range(tail):
            k = h * tail + u
            ew[k, k * HEAD_DIM + entries] = 1
            dw[k, h * LANES + HEAD_DIM] = 1
            for a in range(FEAT):
                eq[h * FEAT + a, k * FEAT + a] = 1
                rq[k * FEAT + a, k] = 1
    return [jnp.asarray(x, BF16) for x in (eq, rq, ew, rv, dw, rn, en, pad)]


def tail_terms(projected, tail_keys, tail_values, tail_length, heads, tail):
    conts = projected.shape[0]
    block = min(conts, 128)
    tables = tail_tables(heads, tail)

    def rows(array):
        return pl.BlockSpec((block, array.shape[1]), lambda i: (i, 0))

    def whole(array):
        return pl.BlockSpec(array.shape, lambda i, n=array.ndim: (0,) * n)

    return pl.pallas_call(
        functools.partial(tail_kernel, heads, tail),
        grid=(conts // block,),
        in_specs=[rows(projected), rows(tail_keys), rows(tail_values), rows(tail_length)]
        + [whole(x) for x in tables],
        out_specs=pl.BlockSpec((block, heads * 2 * LANES), lambda i: (i, 0)),
        out_shape=jax.ShapeDtypeStruct((conts, heads * 2 * LANES), F32),
        compiler_params=pltpu.CompilerParams(vmem_limit_bytes=VMEM_LIMIT),
        cost_estimate=pl.CostEstimate(
            flops=20_000_000_000, bytes_accessed=25_000_000, transcendentals=0
        ),
    )(projected, tail_keys, tail_values, tail_length, *tables)


def combine_kernel(heads, acc_ref, sent_at, kept_at, got_ref, kept_ref, pack, out_ref):
    block = acc_ref.shape[0]
    hd = heads * HEAD_DIM
    sent = sent_at[...] == lax.broadcasted_iota(jnp.int32, (block, got_ref.shape[0]), 1)
    kept = kept_at[...] == lax.broadcasted_iota(jnp.int32, (block, kept_ref.shape[0]), 1)
    sent = sent.astype(F32).astype(BF16)
    kept = kept.astype(F32).astype(BF16)
    prompt = dot(sent, got_ref[...]) + dot(kept, kept_ref[...])
    for t in range(2):
        parts = []
        for h in range(heads):
            at = (2 * h + t) * LANES
            terms = prompt[:, at : at + LANES]
            total = acc_ref[:, at : at + LANES] + terms
            den = total[:, HEAD_DIM : HEAD_DIM + 1]
            den = den + terms[:, HEAD_DIM + 1 : HEAD_DIM + 2] + terms[:, HEAD_DIM + 2 : HEAD_DIM + 3]
            parts.append((total / den).astype(BF16))
        wide = jnp.concatenate(parts, axis=1)
        out_ref[:, t * hd : (t + 1) * hd] = dot(wide, pack[...]).astype(BF16)


def combine(acc, sent_at, kept_at, got, kept, heads):
    conts = acc.shape[0]
    block = min(conts, 128)
    hd = heads * HEAD_DIM
    pack = np.zeros((heads * LANES, hd), np.float32)
    entries = np.arange(HEAD_DIM)
    for h in range(heads):
        pack[h * LANES + entries, h * HEAD_DIM + entries] = 1

    def rows(array):
        return pl.BlockSpec((block, array.shape[1]), lambda i: (i, 0))

    def whole(array):
        return pl.BlockSpec(array.shape, lambda i: (0, 0))

    pack = jnp.asarray(pack, BF16)
    return pl.pallas_call(
        functools.partial(combine_kernel, heads),
        grid=(conts // block,),
        in_specs=[rows(acc), rows(sent_at), rows(kept_at), whole(got), whole(kept), whole(pack)],
        out_specs=pl.BlockSpec((block, 2 * hd), lambda i: (i, 0)),
        out_shape=jax.ShapeDtypeStruct((conts, 2 * hd), BF16),
        compiler_params=pltpu.CompilerParams(vmem_limit_bytes=VMEM_LIMIT),
    )(acc, sent_at, kept_at, got, kept, pack)


def remote(src, dst, send, recv, **target):
    return pltpu.make_async_remote_copy(
        src_ref=src,
        dst_ref=dst,
        send_sem=send,
        recv_sem=recv,
        device_id=target,
        device_id_type=pl.DeviceIdType.MESH,
    )


def greet(targets):
    barrier = pltpu.get_barrier_semaphore()
    for target in targets:
        pl.semaphore_signal(barrier, inc=1, device_id=target, device_id_type=pl.DeviceIdType.MESH)
    pl.semaphore_wait(barrier, len(targets))


def places():
    row, col = lax.axis_index("row"), lax.axis_index("col")
    across = lax.rem(col + 2, 4)
    core = lax.rem(col, 2)
    sibling = col + 1 - 2 * core
    return row, 1 - row, col, across, core, sibling


def front_kernel(
    x, w, tok, wall, via, y_send, y_recv, c_send, c_recv, w_send, w_recv, z_send, z_recv, l_sem
):
    row, partner, col, across, core, sibling = places()
    layer = lax.axis_index("req")
    layers = [lax.rem(layer + k, 4) for k in (1, 2, 3)]
    greet(
        [{"row": partner}]
        + [{"col": lax.rem(col + k, 4)} for k in (1, 2, 3)]
        + [{"req": other} for other in layers]
    )
    parts = c_recv.shape[1]
    chunks = 2 * parts
    size = tok.shape[1] // parts
    quarter = w.shape[0] // 4

    def to_row(j):
        rows = pl.ds(j * size, size)
        return remote(x.at[rows], via.at[rows], y_send.at[j], y_recv.at[j], row=partner)

    def holder_of(source, j):
        return 2 * (row if source == 0 else partner) + j // parts

    def ends(source, j):
        src = (x if source == 0 else via).at[pl.ds(j * size, size)]
        part = j % parts
        return src, tok.at[col, pl.ds(part * size, size)], c_recv.at[col, part]

    def to_holder(source, j):
        src, dst, arrival = ends(source, j)
        return remote(src, dst, c_send.at[source * chunks + j], arrival, col=holder_of(source, j))

    def start_holder(source, j):
        @pl.when(holder_of(source, j) != col)
        def _():
            to_holder(source, j).start()

        @pl.when(holder_of(source, j) == col)
        def _():
            pltpu.make_async_copy(*ends(source, j)).start()

    def rows_of(at):
        return pl.ds(pl.multiple_of(at * quarter, 16), quarter)

    def to_layer(k):
        part = wall.at[across, rows_of(layer)]
        return remote(part, part, z_send.at[k], z_recv.at[k], req=layers[k])

    mine = rows_of(layer)
    w_across = remote(w.at[mine], wall.at[col, mine], w_send.at[0], w_recv.at[0], col=across)
    w_side = remote(w, wall.at[col], w_send.at[1], w_recv.at[1], col=sibling)
    w_on = remote(wall.at[across], wall.at[across], w_send.at[2], w_recv.at[2], col=sibling)
    w_here = pltpu.make_async_copy(w, wall.at[col], l_sem)
    w_across.start()
    for j in range(chunks):
        to_row(j).start()
    for j in range(chunks):
        start_holder(0, j)
    w_side.start()
    w_here.start()
    for j in range(chunks):
        if j == 2:
            got = wall.at[across, mine]
            remote(got, got, w_send.at[0], w_recv.at[0], col=across).wait_recv()
            for k in range(3):
                to_layer(k).start()
        to_row(j).wait_recv()
        start_holder(1, j)
    for k in range(3):
        got = wall.at[across, rows_of(lax.rem(layer + 3 - k, 4))]
        remote(got, got, z_send.at[k], z_recv.at[k], req=layers[k]).wait_recv()
    w_on.start()
    for source in range(2):
        for j in range(chunks):

            @pl.when(holder_of(source, j) != col)
            def _():
                to_holder(source, j).wait_send()

    for k in range(4):
        for part in range(parts):
            rows = pl.ds(part * size, size)

            @pl.when(col != k)
            def _():
                remote(
                    tok.at[k, rows], tok.at[k, rows], c_send.at[0], c_recv.at[k, part], col=across
                ).wait_recv()

            @pl.when(col == k)
            def _():
                pltpu.make_async_copy(tok.at[k, rows], tok.at[k, rows], c_recv.at[k, part]).wait()

    for j in range(chunks):
        to_row(j).wait_send()
    for k in range(3):
        to_layer(k).wait_send()
    w_across.wait_send()
    w_side.wait()
    w_on.wait()
    w_here.wait()


def front(x, w, conts):
    dma = pltpu.SemaphoreType.DMA
    return pl.pallas_call(
        front_kernel,
        in_specs=[pl.BlockSpec(memory_space=pl.ANY)] * 2,
        out_specs=[pl.BlockSpec(memory_space=pl.ANY)] * 3,
        out_shape=[
            jax.ShapeDtypeStruct((4, conts, x.shape[1]), BF16),
            jax.ShapeDtypeStruct((4,) + w.shape, BF16),
            jax.ShapeDtypeStruct(x.shape, BF16),
        ],
        scratch_shapes=[
            dma((8,)), dma((8,)), dma((16,)), dma((4, 4)), dma((3,)), dma((3,)), dma((3,)), dma((3,)), dma,
        ],
        compiler_params=pltpu.CompilerParams(collective_id=0, has_side_effects=True),
    )(x, w)


def back_kernel(h, hall, via, sx, rx, sy, ry, ss, rs, sf, rf, sl):
    row, partner, col, across, core, sibling = places()
    greet([{"row": partner}, {"col": across}, {"col": sibling}])
    pieces = 8
    size = h.shape[0] // pieces
    stays = col // 2 == row

    def at(ref, j):
        return ref.at[pl.ds(j * size, size)]

    def slot(b, half, j):
        return hall.at[b, half, pl.ds(j * size, size)]

    def x_via(j):
        return remote(at(h, j), at(via, j), sx.at[j], rx.at[j], col=across)

    def x_final(j):
        return remote(at(h, j), slot(core, 0, j), sx.at[j], rx.at[j], col=across)

    def y_own(j):
        return remote(at(h, j), slot(core, 1, j), sy.at[j], ry.at[j], row=partner)

    def y_via(j):
        return remote(at(via, j), slot(core, 1, j), sy.at[j], ry.at[j], row=partner)

    def side_own(j):
        return remote(at(h, j), slot(core, 0, j), ss.at[j], rs.at[j], col=sibling)

    def side_got(j):
        return remote(slot(core, 0, j), slot(core, 0, j), ss.at[j], rs.at[j], col=sibling)

    def side_far(j):
        return remote(slot(core, 1, j), slot(core, 1, j), sf.at[j], rf.at[j], col=sibling)

    def keep(j):
        return pltpu.make_async_copy(at(h, j), slot(core, 0, j), sl.at[j])

    for j in range(pieces):

        @pl.when(stays)
        def _():
            x_final(j).start()
            side_own(j).start()
            keep(j).start()

        @pl.when(jnp.logical_not(stays))
        def _():
            x_via(j).start()
            y_own(j).start()

    for j in range(pieces):

        @pl.when(stays)
        def _():
            x_via(j).wait_recv()
            y_via(j).start()

        @pl.when(jnp.logical_not(stays))
        def _():
            remote(slot(core, 0, j), slot(core, 0, j), sx.at[j], rx.at[j], col=across).wait_recv()
            side_got(j).start()

    for j in range(pieces):
        remote(slot(core, 1, j), slot(core, 1, j), sy.at[j], ry.at[j], row=partner).wait_recv()
        side_far(j).start()
    for j in range(pieces):
        near = slot(1 - core, 0, j)
        far = slot(1 - core, 1, j)
        remote(near, near, ss.at[j], rs.at[j], col=sibling).wait_recv()
        remote(far, far, sf.at[j], rf.at[j], col=sibling).wait_recv()
        side_far(j).wait_send()

        @pl.when(stays)
        def _():
            x_final(j).wait_send()
            y_via(j).wait_send()
            side_own(j).wait_send()
            keep(j).wait()

        @pl.when(jnp.logical_not(stays))
        def _():
            x_via(j).wait_send()
            y_own(j).wait_send()
            side_got(j).wait_send()


def back(h):
    dma = pltpu.SemaphoreType.DMA((8,))
    return pl.pallas_call(
        back_kernel,
        in_specs=[pl.BlockSpec(memory_space=pl.ANY)],
        out_specs=[pl.BlockSpec(memory_space=pl.ANY)] * 2,
        out_shape=[
            jax.ShapeDtypeStruct((2, 2) + h.shape, BF16),
            jax.ShapeDtypeStruct(h.shape, BF16),
        ],
        scratch_shapes=[dma] * 9,
        compiler_params=pltpu.CompilerParams(collective_id=1, has_side_effects=True),
    )(h)[0]


def project_kernel(tok_ref, w_ref, out_ref):
    depth, total = w_ref.shape[1:]
    for t in range(2):
        acc = jnp.zeros((tok_ref.shape[1], total), F32)
        for k in range(w_ref.shape[0]):
            acc = acc + dot(tok_ref[k, :, t * depth : (t + 1) * depth], w_ref[k])
        out_ref[:, t * total : (t + 1) * total] = acc.astype(BF16)


def project(tok, w):
    conts, total = tok.shape[1], w.shape[2]
    block = 128
    return pl.pallas_call(
        project_kernel,
        grid=(conts // block,),
        in_specs=[
            pl.BlockSpec((tok.shape[0], block, tok.shape[2]), lambda i: (0, i, 0)),
            pl.BlockSpec(w.shape, lambda i: (0, 0, 0)),
        ],
        out_specs=pl.BlockSpec((block, 2 * total), lambda i: (i, 0)),
        out_shape=jax.ShapeDtypeStruct((conts, 2 * total), BF16),
        compiler_params=pltpu.CompilerParams(vmem_limit_bytes=VMEM_LIMIT),
    )(tok, w)


def output_kernel(h_ref, w_ref, x_ref, out_ref):
    hd, depth = w_ref.shape[1:]
    for t in range(2):
        acc = x_ref[:, t * depth : (t + 1) * depth].astype(F32)
        for half in range(2):
            part = dot(h_ref[0, half, :, t * hd : (t + 1) * hd], w_ref[half])
            acc = acc + part.astype(BF16).astype(F32)
        out_ref[:, t * depth : (t + 1) * depth] = acc.astype(BF16)


def output(hall, w, flat):
    block = 128
    steps = hall.shape[2] // block
    return pl.pallas_call(
        output_kernel,
        grid=(2, steps),
        in_specs=[
            pl.BlockSpec((1, 2, block, hall.shape[3]), lambda b, i: (b, 0, i, 0)),
            pl.BlockSpec(w.shape, lambda b, i: (0, 0, 0)),
            pl.BlockSpec((block, flat.shape[1]), lambda b, i: (b * steps + i, 0)),
        ],
        out_specs=pl.BlockSpec((block, flat.shape[1]), lambda b, i: (b * steps + i, 0)),
        out_shape=jax.ShapeDtypeStruct(flat.shape, BF16),
        compiler_params=pltpu.CompilerParams(vmem_limit_bytes=VMEM_LIMIT),
    )(hall, w, flat)


def body(
    tokens,
    w_query,
    w_key,
    w_value,
    w_out,
    cached_state,
    cached_norm,
    slot_prompt,
    prompt_of,
    tail_keys,
    tail_values,
    tail_length,
):
    heads = w_query.shape[1] // FEAT
    depth = w_query.shape[0]
    hf, hd = heads * FEAT, heads * HEAD_DIM
    slots = slot_prompt.shape[0]
    conts = prompt_of.shape[0]
    per = conts // slots
    tail = tail_keys.shape[1] // hf
    axes = ("req", "col")
    holders = lax.axis_size(axes)
    capacity = (slots // 2 + holders - 2) // (holders - 1)
    me = lax.axis_index(axes)

    copies = jnp.broadcast_to(slot_prompt[None, None], (holders, 1, slots))
    every = lax.all_to_all(copies, axes, split_axis=0, concat_axis=0, tiled=True).reshape(-1)
    flat = tokens.reshape(tokens.shape[0], 2 * depth)
    value_weight = jnp.moveaxis(w_value.reshape(heads, depth, HEAD_DIM), 0, 1).reshape(depth, hd)
    stacked = jnp.concatenate([w_query, w_key, value_weight], axis=1)
    direct = lax.axis_size("row") == 2 and lax.axis_size("col") == lax.axis_size("req") == 4
    if direct:
        tok, w_all, _ = front(flat, stacked, conts)
        projected, wo_own = lax.optimization_barrier((project(tok, w_all), w_out))
        wo_all = jnp.stack([wo_own, lax.ppermute(wo_own, "row", [(0, 1), (1, 0)])])
    else:
        gathered = lax.all_gather(flat, "row", axis=0, tiled=True)
        partial_sums = [
            dot(gathered[:, t * depth : (t + 1) * depth], stacked).astype(BF16) for t in range(2)
        ]
        projected = lax.psum_scatter(
            jnp.concatenate(partial_sums, axis=1), "col", scatter_dimension=0, tiled=True
        )
    states = turn_states(cached_state, jnp.transpose(cached_norm, (2, 0, 1)), heads, slots)

    owner = (every // slots).reshape(holders, slots)
    before = jnp.arange(slots)[None, :] < jnp.arange(slots)[:, None]
    position = jnp.sum((owner[:, :, None] == owner[:, None, :]) & before[None], axis=2).reshape(-1)
    block_of = jnp.arange(holders * slots, dtype=jnp.int32) // slots * capacity + position
    local = prompt_of - me * slots
    found = prompt_of[:, None] == every[None, :]
    slot_at = jnp.max(jnp.where(found, jnp.arange(holders * slots, dtype=jnp.int32)[None, :], 0), axis=1)
    block_at = jnp.max(jnp.where(found, block_of[None, :], 0), axis=1)
    same = local[:, None] == local[None, :]
    rank = jnp.sum(same & (jnp.arange(conts)[None, :] < jnp.arange(conts)[:, None]), axis=1)
    away = slot_at // slots != me
    sent_at = jnp.where(away, block_at * per + rank, -1).astype(jnp.int32)
    kept_at = jnp.where(away, -1, slot_at % slots * per + rank).astype(jnp.int32)
    slot_owner = slot_prompt // slots
    mine_before = (slot_owner[:, None] == slot_owner[None, :]) & before
    slot_block = slot_owner * capacity + jnp.sum(mine_before, axis=1)
    slot_block = jnp.where(slot_owner == me, -1, slot_block)
    served = jnp.where(
        slot_block[:, None] < 0, -1, slot_block[:, None] * per + jnp.arange(per)[None, :]
    ).reshape(-1)
    sends = jnp.arange(holders * capacity * per)

    total = 2 * hf + hd
    queries = jnp.concatenate([projected[:, :hf], projected[:, total : total + hf]], axis=1)
    outgoing = dot((sends[:, None] == sent_at[None, :]).astype(BF16), queries).astype(BF16)
    incoming = lax.all_to_all(
        outgoing.reshape(holders, capacity * per, 2 * hf), axes, split_axis=0, concat_axis=0, tiled=True
    ).reshape(-1, 2 * hf)
    acc = tail_terms(projected, tail_keys, tail_values, tail_length[:, None], heads, tail)
    kept_queries = dot((jnp.arange(conts)[:, None] == kept_at[None, :]).astype(BF16), queries)
    slot_queries = dot((served[:, None] == sends[None, :]).astype(BF16), incoming) + kept_queries
    prompt = prompt_terms(slot_queries.astype(BF16), states, heads, slots)
    replies = dot((sends[:, None] == served[None, :]).astype(BF16), prompt).astype(BF16)
    answers = lax.all_to_all(
        replies.reshape(holders, capacity * per, -1), axes, split_axis=0, concat_axis=0, tiled=True
    ).reshape(replies.shape)
    heads_out = combine(acc, sent_at[:, None], kept_at[:, None], answers, prompt, heads)

    if direct:
        return output(back(heads_out), wo_all, flat).reshape(tokens.shape)
    everyone = lax.all_gather(heads_out, "col", axis=0, tiled=True)
    terms = jnp.concatenate(
        [dot(everyone[:, t * hd : (t + 1) * hd], w_out).astype(BF16) for t in range(2)], axis=1
    )
    mixed = lax.psum_scatter(terms, "row", scatter_dimension=0, tiled=True)
    return (mixed.astype(F32) + flat.astype(F32)).astype(BF16).reshape(tokens.shape)


def solution(mesh):
    return jax.shard_map(
        body,
        mesh=mesh,
        in_specs=(
            P(("req", "row"), None, "col"),
            P("col", "row"),
            P("col", "row"),
            P("row", "col"),
            P("row", "col"),
            P(("req", "col"), None, "row"),
            P(("req", "col"), None, "row"),
            P(("req", "col")),
            P(("req", "col")),
            P(("req", "col"), "row"),
            P(("req", "col"), "row"),
            P(("req", "col")),
        ),
        out_specs=P(("req", "row"), None, "col"),
        check_vma=False,
    )
```

```python
import functools

import jax
import jax.numpy as jnp
import numpy as np
from jax import lax
from jax.experimental import pallas as pl
from jax.experimental.pallas import tpu as pltpu
from jax.sharding import PartitionSpec as P

FEAT = 16
HEAD_DIM = 112
LANES = 128
TAYLOR_PAD = 384
F32 = jnp.float32
BF16 = jnp.bfloat16
VMEM_LIMIT = 48 * 1024 * 1024
CONTRACT_LAST = (((1,), (1,)), ((), ()))


def dot(a, b):
    return jnp.dot(a, b, preferred_element_type=F32)


def kappa(s):
    return 1.0 + s + 0.5 * s * s


def split3(x):
    hi = x.astype(BF16)
    rest = x - hi.astype(F32)
    mid = rest.astype(BF16)
    return hi, mid, (rest - mid.astype(F32)).astype(BF16)


def state_kernel(perm_ref, state_ref, norm_ref, out_ref):
    slots = out_ref.shape[1]
    taylor = state_ref.shape[1]
    width = 8 * slots
    perm = perm_ref[...]
    out_ref[0, :, :, taylor:] = jnp.zeros((slots, LANES, TAYLOR_PAD - taylor), BF16)
    for pair in range(HEAD_DIM // 16):
        parts = []
        for half in range(2):
            lower = (2 * pair + half) * width
            turned = lax.dot_general(
                perm, state_ref[0, :, lower : lower + width], CONTRACT_LAST, preferred_element_type=F32
            )
            parts.append(turned.reshape(slots, 8, taylor))
        both = jnp.concatenate(parts, axis=1).astype(BF16)
        out_ref[0, :, pair * 16 : pair * 16 + 16, :taylor] = both
    norm = norm_ref[0].astype(F32)
    wide = jnp.broadcast_to(norm[:, None, :], (slots, 16, taylor)).astype(BF16)
    out_ref[0, :, HEAD_DIM:, :taylor] = wide


def turn_states(cached_state, norm, heads, slots):
    taylor = cached_state.shape[1]
    width = 8 * slots
    perm = np.zeros((width, width), np.float32)
    for v in range(8):
        for q in range(slots):
            perm[q * 8 + v, v * slots + q] = 1
    return pl.pallas_call(
        state_kernel,
        grid=(heads,),
        in_specs=[
            pl.BlockSpec((width, width), lambda h: (0, 0)),
            pl.BlockSpec((1, taylor, HEAD_DIM * slots), lambda h: (0, 0, h)),
            pl.BlockSpec((1, slots, taylor), lambda h: (h, 0, 0)),
        ],
        out_specs=pl.BlockSpec((1, slots, LANES, TAYLOR_PAD), lambda h: (h, 0, 0, 0)),
        out_shape=jax.ShapeDtypeStruct((heads, slots, LANES, TAYLOR_PAD), BF16),
        compiler_params=pltpu.CompilerParams(vmem_limit_bytes=VMEM_LIMIT),
        cost_estimate=pl.CostEstimate(
            flops=20_000_000_000, bytes_accessed=45_000_000, transcendentals=0
        ),
    )(jnp.asarray(perm, BF16), cached_state, norm)


def prompt_kernel(q_ref, pick_ref, shift_ref, states_ref, out_ref, phi_ref):
    rows = q_ref.shape[0]
    slots = states_ref.shape[1]
    per = rows // slots
    width = q_ref.shape[1] // 2
    pick = pick_ref[0]
    for t in range(2):
        both = dot(q_ref[:, t * width : (t + 1) * width], pick)
        left = both[:, :TAYLOR_PAD] + shift_ref[0:1]
        right = both[:, TAYLOR_PAD:] + shift_ref[1:2]
        phi = left * right * shift_ref[2:3]
        hi = phi.astype(BF16)
        phi_ref[t] = hi
        phi_ref[2 + t] = (phi - hi.astype(F32)).astype(BF16)
    lane = lax.broadcasted_iota(jnp.int32, (2 * per, LANES), 1)
    for q in range(slots):
        pieces = [phi_ref[k, q * per : (q + 1) * per, :] for k in range(4)]
        got = lax.dot_general(
            jnp.concatenate(pieces, axis=0), states_ref[0, q], CONTRACT_LAST, preferred_element_type=F32
        )
        top = got[: 2 * per]
        den = top + got[2 * per :]
        hi, mid, low = split3(den)
        res = jnp.where(lane < HEAD_DIM, top, hi.astype(F32))
        res = jnp.where(lane == HEAD_DIM + 1, mid.astype(F32), res)
        res = jnp.where(lane == HEAD_DIM + 2, low.astype(F32), res).astype(BF16)
        out_ref[q * per : (q + 1) * per, :LANES] = res[:per]
        out_ref[q * per : (q + 1) * per, LANES:] = res[per:]


def pick_tables(heads):
    pick = np.zeros((heads, heads * FEAT, 2 * TAYLOR_PAD), np.float32)
    shift = np.zeros((8, TAYLOR_PAD), np.float32)
    shift[0, 0] = 1
    shift[1, : FEAT + 1] = 1
    shift[2, 0] = 1
    shift[2, 1 : FEAT + 1] = FEAT ** (-0.25)
    shift[2, FEAT + 1 : FEAT + 1 + FEAT * FEAT] = 0.5**0.5 / FEAT**0.5
    for h in range(heads):
        for a in range(FEAT):
            pick[h, h * FEAT + a, 1 + a] = 1
            for b in range(FEAT):
                f = 1 + FEAT + a * FEAT + b
                pick[h, h * FEAT + a, f] = 1
                pick[h, h * FEAT + b, TAYLOR_PAD + f] = 1
    return jnp.asarray(pick, BF16), jnp.asarray(shift, F32)


def prompt_terms(slot_queries, states, heads, slots):
    rows = slot_queries.shape[0]
    pick, shift = pick_tables(heads)
    return pl.pallas_call(
        prompt_kernel,
        grid=(heads,),
        in_specs=[
            pl.BlockSpec(slot_queries.shape, lambda h: (0, 0)),
            pl.BlockSpec((1,) + pick.shape[1:], lambda h: (h, 0, 0)),
            pl.BlockSpec(shift.shape, lambda h: (0, 0)),
            pl.BlockSpec((1, slots, LANES, TAYLOR_PAD), lambda h: (h, 0, 0, 0)),
        ],
        out_specs=pl.BlockSpec((rows, 2 * LANES), lambda h: (0, h)),
        out_shape=jax.ShapeDtypeStruct((rows, heads * 2 * LANES), BF16),
        scratch_shapes=[pltpu.VMEM((4, rows, TAYLOR_PAD), BF16)],
        compiler_params=pltpu.CompilerParams(vmem_limit_bytes=VMEM_LIMIT),
    )(slot_queries, pick, shift, states)


def tail_kernel(heads, tail, q_ref, tk_ref, tv_ref, len_ref, eq, rq, ew, rv, dw, rn, en, pad, out_ref):
    hf = heads * FEAT
    hd = heads * HEAD_DIM
    total = 2 * hf + hd
    block = q_ref.shape[0]
    lane = lax.broadcasted_iota(jnp.int32, (block, heads * tail), 1)
    live = lax.rem(lane, tail) < len_ref[...]
    keys = tk_ref[...].astype(F32)
    scale = FEAT ** (-0.5)
    new_k = [q_ref[:, t * total + hf : t * total + 2 * hf].astype(F32) for t in range(2)]
    new_v = [dot(q_ref[:, t * total + 2 * hf : (t + 1) * total], pad[...]) for t in range(2)]
    for t in range(2):
        query = q_ref[:, t * total : t * total + hf]
        spread = dot(query, eq[...])
        scores = dot((spread * keys).astype(BF16), rq[...]) * scale
        weight = jnp.where(live, kappa(scores), 0.0)
        hi = weight.astype(BF16)
        low = (weight - hi.astype(F32)).astype(BF16)
        acc = dot(hi, dw[...]) + dot(low, dw[...])
        for i in range(t + 1):
            product = (query.astype(F32) * new_k[i]).astype(BF16)
            fresh = kappa(dot(product, rn[...]) * scale)
            fresh_hi = fresh.astype(BF16)
            fresh_low = (fresh - fresh_hi.astype(F32)).astype(BF16)
            spread_hi = dot(fresh_hi, en[0])
            acc = acc + spread_hi * new_v[i] + dot(fresh_hi, en[1]) + dot(fresh_low, en[1])
        span = tail * HEAD_DIM
        for h in range(heads):
            wide = dot(hi, ew[:, h * span : (h + 1) * span])
            product = wide * tv_ref[:, h * span : (h + 1) * span].astype(F32)
            summed = dot(product.astype(BF16), rv[...])
            at = (2 * h + t) * LANES
            out_ref[:, at : at + LANES] = acc[:, h * LANES : (h + 1) * LANES] + summed


def tail_tables(heads, tail):
    hf, hd = heads * FEAT, heads * HEAD_DIM
    eq = np.zeros((hf, heads * tail * FEAT), np.float32)
    rq = np.zeros((heads * tail * FEAT, heads * tail), np.float32)
    ew = np.zeros((heads * tail, heads * tail * HEAD_DIM), np.float32)
    rv = np.zeros((tail * HEAD_DIM, LANES), np.float32)
    dw = np.zeros((heads * tail, heads * LANES), np.float32)
    rn = np.zeros((hf, LANES), np.float32)
    en = np.zeros((2, LANES, heads * LANES), np.float32)
    pad = np.zeros((hd, heads * LANES), np.float32)
    entries = np.arange(HEAD_DIM)
    for u in range(tail):
        rv[u * HEAD_DIM + entries, entries] = 1
    for h in range(heads):
        en[0, h, h * LANES + entries] = 1
        en[1, h, h * LANES + HEAD_DIM] = 1
        pad[h * HEAD_DIM + entries, h * LANES + entries] = 1
        rn[h * FEAT : (h + 1) * FEAT, h] = 1
        for u in range(tail):
            k = h * tail + u
            ew[k, k * HEAD_DIM + entries] = 1
            dw[k, h * LANES + HEAD_DIM] = 1
            for a in range(FEAT):
                eq[h * FEAT + a, k * FEAT + a] = 1
                rq[k * FEAT + a, k] = 1
    return [jnp.asarray(x, BF16) for x in (eq, rq, ew, rv, dw, rn, en, pad)]


def tail_terms(projected, tail_keys, tail_values, tail_length, heads, tail):
    conts = projected.shape[0]
    block = min(conts, 128)
    tables = tail_tables(heads, tail)

    def rows(array):
        return pl.BlockSpec((block, array.shape[1]), lambda i: (i, 0))

    def whole(array):
        return pl.BlockSpec(array.shape, lambda i, n=array.ndim: (0,) * n)

    return pl.pallas_call(
        functools.partial(tail_kernel, heads, tail),
        grid=(conts // block,),
        in_specs=[rows(projected), rows(tail_keys), rows(tail_values), rows(tail_length)]
        + [whole(x) for x in tables],
        out_specs=pl.BlockSpec((block, heads * 2 * LANES), lambda i: (i, 0)),
        out_shape=jax.ShapeDtypeStruct((conts, heads * 2 * LANES), F32),
        compiler_params=pltpu.CompilerParams(vmem_limit_bytes=VMEM_LIMIT),
        cost_estimate=pl.CostEstimate(
            flops=20_000_000_000, bytes_accessed=25_000_000, transcendentals=0
        ),
    )(projected, tail_keys, tail_values, tail_length, *tables)


def combine_kernel(heads, acc_ref, sent_at, kept_at, got_ref, kept_ref, pack, out_ref):
    block = acc_ref.shape[0]
    hd = heads * HEAD_DIM
    sent = sent_at[...] == lax.broadcasted_iota(jnp.int32, (block, got_ref.shape[0]), 1)
    kept = kept_at[...] == lax.broadcasted_iota(jnp.int32, (block, kept_ref.shape[0]), 1)
    sent = sent.astype(F32).astype(BF16)
    kept = kept.astype(F32).astype(BF16)
    prompt = dot(sent, got_ref[...]) + dot(kept, kept_ref[...])
    for t in range(2):
        parts = []
        for h in range(heads):
            at = (2 * h + t) * LANES
            terms = prompt[:, at : at + LANES]
            total = acc_ref[:, at : at + LANES] + terms
            den = total[:, HEAD_DIM : HEAD_DIM + 1]
            den = den + terms[:, HEAD_DIM + 1 : HEAD_DIM + 2] + terms[:, HEAD_DIM + 2 : HEAD_DIM + 3]
            parts.append((total / den).astype(BF16))
        wide = jnp.concatenate(parts, axis=1)
        out_ref[:, t * hd : (t + 1) * hd] = dot(wide, pack[...]).astype(BF16)


def pack_table(heads):
    pack = np.zeros((heads * LANES, heads * HEAD_DIM), np.float32)
    entries = np.arange(HEAD_DIM)
    for h in range(heads):
        pack[h * LANES + entries, h * HEAD_DIM + entries] = 1
    return jnp.asarray(pack, BF16)


def combine(acc, sent_at, kept_at, got, kept, heads):
    conts = acc.shape[0]
    block = min(conts, 128)
    hd = heads * HEAD_DIM

    def rows(array):
        return pl.BlockSpec((block, array.shape[1]), lambda i: (i, 0))

    def whole(array):
        return pl.BlockSpec(array.shape, lambda i: (0, 0))

    pack = pack_table(heads)
    return pl.pallas_call(
        functools.partial(combine_kernel, heads),
        grid=(conts // block,),
        in_specs=[rows(acc), rows(sent_at), rows(kept_at), whole(got), whole(kept), whole(pack)],
        out_specs=pl.BlockSpec((block, 2 * hd), lambda i: (i, 0)),
        out_shape=jax.ShapeDtypeStruct((conts, 2 * hd), BF16),
        compiler_params=pltpu.CompilerParams(vmem_limit_bytes=VMEM_LIMIT),
    )(acc, sent_at, kept_at, got, kept, pack)


def remote(src, dst, send, recv, **target):
    return pltpu.make_async_remote_copy(
        src_ref=src,
        dst_ref=dst,
        send_sem=send,
        recv_sem=recv,
        device_id=target,
        device_id_type=pl.DeviceIdType.MESH,
    )


def greet(targets):
    barrier = pltpu.get_barrier_semaphore()
    for target in targets:
        pl.semaphore_signal(barrier, inc=1, device_id=target, device_id_type=pl.DeviceIdType.MESH)
    pl.semaphore_wait(barrier, len(targets))


def places():
    row, col = lax.axis_index("row"), lax.axis_index("col")
    across = lax.rem(col + 2, 4)
    core = lax.rem(col, 2)
    sibling = col + 1 - 2 * core
    return row, 1 - row, col, across, core, sibling


def front_kernel(
    x, w, tok, wall, via, y_send, y_recv, c_send, c_recv, w_send, w_recv, z_send, z_recv, l_sem
):
    row, partner, col, across, core, sibling = places()
    layer = lax.axis_index("req")
    layers = [lax.rem(layer + k, 4) for k in (1, 2, 3)]
    greet(
        [{"row": partner}]
        + [{"col": lax.rem(col + k, 4)} for k in (1, 2, 3)]
        + [{"req": other} for other in layers]
    )
    parts = c_recv.shape[1]
    chunks = 2 * parts
    size = tok.shape[1] // parts
    quarter = w.shape[0] // 4

    def to_row(j):
        rows = pl.ds(j * size, size)
        return remote(x.at[rows], via.at[rows], y_send.at[j], y_recv.at[j], row=partner)

    def holder_of(source, j):
        return 2 * (row if source == 0 else partner) + j // parts

    def ends(source, j):
        src = (x if source == 0 else via).at[pl.ds(j * size, size)]
        part = j % parts
        return src, tok.at[col, pl.ds(part * size, size)], c_recv.at[col, part]

    def to_holder(source, j):
        src, dst, arrival = ends(source, j)
        return remote(src, dst, c_send.at[source * chunks + j], arrival, col=holder_of(source, j))

    def start_holder(source, j):
        @pl.when(holder_of(source, j) != col)
        def _():
            to_holder(source, j).start()

        @pl.when(holder_of(source, j) == col)
        def _():
            pltpu.make_async_copy(*ends(source, j)).start()

    def rows_of(at):
        return pl.ds(pl.multiple_of(at * quarter, 16), quarter)

    def to_layer(k):
        part = wall.at[across, rows_of(layer)]
        return remote(part, part, z_send.at[k], z_recv.at[k], req=layers[k])

    mine = rows_of(layer)
    w_across = remote(w.at[mine], wall.at[col, mine], w_send.at[0], w_recv.at[0], col=across)
    w_side = remote(w, wall.at[col], w_send.at[1], w_recv.at[1], col=sibling)
    w_on = remote(wall.at[across], wall.at[across], w_send.at[2], w_recv.at[2], col=sibling)
    w_here = pltpu.make_async_copy(w, wall.at[col], l_sem)
    w_across.start()
    for j in range(chunks):
        to_row(j).start()
    for j in range(chunks):
        start_holder(0, j)
    w_side.start()
    w_here.start()
    for j in range(chunks):
        if j == 2:
            got = wall.at[across, mine]
            remote(got, got, w_send.at[0], w_recv.at[0], col=across).wait_recv()
            for k in range(3):
                to_layer(k).start()
        to_row(j).wait_recv()
        start_holder(1, j)
    for k in range(3):
        got = wall.at[across, rows_of(lax.rem(layer + 3 - k, 4))]
        remote(got, got, z_send.at[k], z_recv.at[k], req=layers[k]).wait_recv()
    w_on.start()
    for source in range(2):
        for j in range(chunks):

            @pl.when(holder_of(source, j) != col)
            def _():
                to_holder(source, j).wait_send()

    for k in range(4):
        for part in range(parts):
            rows = pl.ds(part * size, size)

            @pl.when(col != k)
            def _():
                remote(
                    tok.at[k, rows], tok.at[k, rows], c_send.at[0], c_recv.at[k, part], col=across
                ).wait_recv()

            @pl.when(col == k)
            def _():
                pltpu.make_async_copy(tok.at[k, rows], tok.at[k, rows], c_recv.at[k, part]).wait()

    for j in range(chunks):
        to_row(j).wait_send()
    for k in range(3):
        to_layer(k).wait_send()
    w_across.wait_send()
    w_side.wait()
    w_on.wait()
    w_here.wait()


def front(x, w, conts):
    dma = pltpu.SemaphoreType.DMA
    return pl.pallas_call(
        front_kernel,
        in_specs=[pl.BlockSpec(memory_space=pl.ANY)] * 2,
        out_specs=[pl.BlockSpec(memory_space=pl.ANY)] * 3,
        out_shape=[
            jax.ShapeDtypeStruct((4, conts, x.shape[1]), BF16),
            jax.ShapeDtypeStruct((4,) + w.shape, BF16),
            jax.ShapeDtypeStruct(x.shape, BF16),
        ],
        scratch_shapes=[
            dma((8,)), dma((8,)), dma((16,)), dma((4, 4)), dma((3,)), dma((3,)), dma((3,)), dma((3,)), dma,
        ],
        compiler_params=pltpu.CompilerParams(collective_id=0, has_side_effects=True),
    )(x, w)


def back_kernel(
    heads, acc, sent_at, kept_at, got, kept, pack, w, x, out, h, hall, via, sx, rx, sy, ry, ss, rs, sf, rf, sl
):
    row, partner, col, across, core, sibling = places()
    greet([{"row": partner}, {"col": across}, {"col": sibling}])
    pieces = 8
    size = h.shape[0] // pieces
    stays = col // 2 == row

    def at(ref, j):
        return ref.at[pl.ds(pl.multiple_of(j * size, size), size)]

    def slot(b, half, j):
        return hall.at[b, half, pl.ds(pl.multiple_of(j * size, size), size)]

    def x_via(j):
        return remote(at(h, j), at(via, j), sx.at[j], rx.at[j], col=across)

    def x_final(j):
        return remote(at(h, j), slot(core, 0, j), sx.at[j], rx.at[j], col=across)

    def y_own(j):
        return remote(at(h, j), slot(core, 1, j), sy.at[j], ry.at[j], row=partner)

    def y_via(j):
        return remote(at(via, j), slot(core, 1, j), sy.at[j], ry.at[j], row=partner)

    def side_own(j):
        return remote(at(h, j), slot(core, 0, j), ss.at[j], rs.at[j], col=sibling)

    def side_got(j):
        return remote(slot(core, 0, j), slot(core, 0, j), ss.at[j], rs.at[j], col=sibling)

    def side_far(j):
        return remote(slot(core, 1, j), slot(core, 1, j), sf.at[j], rf.at[j], col=sibling)

    def keep(j):
        return pltpu.make_async_copy(at(h, j), slot(core, 0, j), sl.at[j])

    block = 2 * size
    count = pieces // 2

    def sums(i, carry):
        rows = pl.ds(pl.multiple_of(i * block, block), block)
        parts = [acc.at[rows], sent_at.at[rows], kept_at.at[rows]]
        combine_kernel(heads, *parts, got, kept, pack, h.at[rows])
        for extra in range(2):
            j = 2 * i + extra

            @pl.when(stays)
            def _():
                x_final(j).start()
                side_own(j).start()
                keep(j).start()

            @pl.when(jnp.logical_not(stays))
            def _():
                x_via(j).start()
                y_own(j).start()

        return carry

    lax.fori_loop(0, count, sums, 0)
    for j in range(pieces):

        @pl.when(stays)
        def _():
            x_via(j).wait_recv()
            y_via(j).start()

        @pl.when(jnp.logical_not(stays))
        def _():
            remote(slot(core, 0, j), slot(core, 0, j), sx.at[j], rx.at[j], col=across).wait_recv()
            side_got(j).start()

    hd, depth = w.shape[1:]

    def products(i):
        for j in (2 * i, 2 * i + 1):
            near, far = slot(1 - core, 0, j), slot(1 - core, 1, j)
            remote(near, near, ss.at[j], rs.at[j], col=sibling).wait_recv()
            remote(far, far, sf.at[j], rf.at[j], col=sibling).wait_recv()

            @pl.when(stays)
            def _():
                keep(j).wait()

        rows = pl.ds(i * block, block)
        for b in range(2):
            place = pl.ds(b * h.shape[0] + i * block, block)
            for t in range(2):
                total = x[place, t * depth : (t + 1) * depth].astype(F32)
                for half in range(2):
                    part = dot(hall[b, half, rows, t * hd : (t + 1) * hd], w[half])
                    total = total + part.astype(BF16).astype(F32)
                out[place, t * depth : (t + 1) * depth] = total.astype(BF16)

    for i in range(count):
        for j in (2 * i, 2 * i + 1):
            far = slot(core, 1, j)
            remote(far, far, sy.at[j], ry.at[j], row=partner).wait_recv()
            side_far(j).start()
        if i > 0:
            products(i - 1)
    products(count - 1)
    for j in range(pieces):
        side_far(j).wait_send()

        @pl.when(stays)
        def _():
            x_final(j).wait_send()
            y_via(j).wait_send()
            side_own(j).wait_send()

        @pl.when(jnp.logical_not(stays))
        def _():
            x_via(j).wait_send()
            y_own(j).wait_send()
            side_got(j).wait_send()


def back(acc, sent_at, kept_at, got, kept, w, flat, heads):
    dma = pltpu.SemaphoreType.DMA((8,))
    conts, hd = acc.shape[0], heads * HEAD_DIM
    wide = (conts, 2 * hd)
    return pl.pallas_call(
        functools.partial(back_kernel, heads),
        in_specs=[pl.BlockSpec(memory_space=pltpu.VMEM)] * 8,
        out_specs=pl.BlockSpec(memory_space=pltpu.VMEM),
        out_shape=jax.ShapeDtypeStruct(flat.shape, BF16),
        scratch_shapes=[pltpu.VMEM(wide, BF16), pltpu.VMEM((2, 2) + wide, BF16), pltpu.VMEM(wide, BF16)]
        + [dma] * 9,
        compiler_params=pltpu.CompilerParams(
            collective_id=1, has_side_effects=True, vmem_limit_bytes=VMEM_LIMIT
        ),
    )(acc, sent_at, kept_at, got, kept, pack_table(heads), w, flat)


def project_kernel(tok_ref, w_ref, out_ref):
    depth, total = w_ref.shape[1:]
    for t in range(2):
        acc = jnp.zeros((tok_ref.shape[1], total), F32)
        for k in range(w_ref.shape[0]):
            acc = acc + dot(tok_ref[k, :, t * depth : (t + 1) * depth], w_ref[k])
        out_ref[:, t * total : (t + 1) * total] = acc.astype(BF16)


def project(tok, w):
    conts, total = tok.shape[1], w.shape[2]
    block = 128
    return pl.pallas_call(
        project_kernel,
        grid=(conts // block,),
        in_specs=[
            pl.BlockSpec((tok.shape[0], block, tok.shape[2]), lambda i: (0, i, 0)),
            pl.BlockSpec(w.shape, lambda i: (0, 0, 0)),
        ],
        out_specs=pl.BlockSpec((block, 2 * total), lambda i: (i, 0)),
        out_shape=jax.ShapeDtypeStruct((conts, 2 * total), BF16),
        compiler_params=pltpu.CompilerParams(vmem_limit_bytes=VMEM_LIMIT),
    )(tok, w)


def body(
    tokens,
    w_query,
    w_key,
    w_value,
    w_out,
    cached_state,
    cached_norm,
    slot_prompt,
    prompt_of,
    tail_keys,
    tail_values,
    tail_length,
):
    heads = w_query.shape[1] // FEAT
    depth = w_query.shape[0]
    hf, hd = heads * FEAT, heads * HEAD_DIM
    slots = slot_prompt.shape[0]
    conts = prompt_of.shape[0]
    per = conts // slots
    tail = tail_keys.shape[1] // hf
    axes = ("req", "col")
    holders = lax.axis_size(axes)
    capacity = (slots // 2 + holders - 2) // (holders - 1)
    me = lax.axis_index(axes)

    copies = jnp.broadcast_to(slot_prompt[None, None], (holders, 1, slots))
    every = lax.all_to_all(copies, axes, split_axis=0, concat_axis=0, tiled=True).reshape(-1)
    flat = tokens.reshape(tokens.shape[0], 2 * depth)
    value_weight = jnp.moveaxis(w_value.reshape(heads, depth, HEAD_DIM), 0, 1).reshape(depth, hd)
    stacked = jnp.concatenate([w_query, w_key, value_weight], axis=1)
    direct = lax.axis_size("row") == 2 and lax.axis_size("col") == lax.axis_size("req") == 4
    if direct:
        tok, w_all, _ = front(flat, stacked, conts)
        projected, wo_own = lax.optimization_barrier((project(tok, w_all), w_out))
        wo_all = jnp.stack([wo_own, lax.ppermute(wo_own, "row", [(0, 1), (1, 0)])])
    else:
        gathered = lax.all_gather(flat, "row", axis=0, tiled=True)
        partial_sums = [
            dot(gathered[:, t * depth : (t + 1) * depth], stacked).astype(BF16) for t in range(2)
        ]
        projected = lax.psum_scatter(
            jnp.concatenate(partial_sums, axis=1), "col", scatter_dimension=0, tiled=True
        )

    owner = (every // slots).reshape(holders, slots)
    before = jnp.arange(slots)[None, :] < jnp.arange(slots)[:, None]
    position = jnp.sum((owner[:, :, None] == owner[:, None, :]) & before[None], axis=2).reshape(-1)
    block_of = jnp.arange(holders * slots, dtype=jnp.int32) // slots * capacity + position
    local = prompt_of - me * slots
    found = prompt_of[:, None] == every[None, :]
    slot_at = jnp.max(jnp.where(found, jnp.arange(holders * slots, dtype=jnp.int32)[None, :], 0), axis=1)
    block_at = jnp.max(jnp.where(found, block_of[None, :], 0), axis=1)
    same = local[:, None] == local[None, :]
    rank = jnp.sum(same & (jnp.arange(conts)[None, :] < jnp.arange(conts)[:, None]), axis=1)
    away = slot_at // slots != me
    sent_at = jnp.where(away, block_at * per + rank, -1).astype(jnp.int32)
    kept_at = jnp.where(away, -1, slot_at % slots * per + rank).astype(jnp.int32)
    slot_owner = slot_prompt // slots
    mine_before = (slot_owner[:, None] == slot_owner[None, :]) & before
    slot_block = slot_owner * capacity + jnp.sum(mine_before, axis=1)
    slot_block = jnp.where(slot_owner == me, -1, slot_block)
    served = jnp.where(
        slot_block[:, None] < 0, -1, slot_block[:, None] * per + jnp.arange(per)[None, :]
    ).reshape(-1)
    sends = jnp.arange(holders * capacity * per)

    total = 2 * hf + hd
    queries = jnp.concatenate([projected[:, :hf], projected[:, total : total + hf]], axis=1)
    outgoing = dot((sends[:, None] == sent_at[None, :]).astype(BF16), queries).astype(BF16)
    norm, outgoing = lax.optimization_barrier((jnp.transpose(cached_norm, (2, 0, 1)), outgoing))
    states = turn_states(cached_state, norm, heads, slots)
    incoming = lax.all_to_all(
        outgoing.reshape(holders, capacity * per, 2 * hf), axes, split_axis=0, concat_axis=0, tiled=True
    ).reshape(-1, 2 * hf)
    acc = tail_terms(projected, tail_keys, tail_values, tail_length[:, None], heads, tail)
    kept_queries = dot((jnp.arange(conts)[:, None] == kept_at[None, :]).astype(BF16), queries)
    slot_queries = dot((served[:, None] == sends[None, :]).astype(BF16), incoming) + kept_queries
    prompt = prompt_terms(slot_queries.astype(BF16), states, heads, slots)
    replies = dot((sends[:, None] == served[None, :]).astype(BF16), prompt).astype(BF16)
    answers = lax.all_to_all(
        replies.reshape(holders, capacity * per, -1), axes, split_axis=0, concat_axis=0, tiled=True
    ).reshape(replies.shape)
    sums = (acc, sent_at[:, None], kept_at[:, None], answers, prompt)
    if direct:
        return back(*sums, wo_all, flat, heads).reshape(tokens.shape)
    heads_out = combine(*sums, heads)

    everyone = lax.all_gather(heads_out, "col", axis=0, tiled=True)
    terms = jnp.concatenate(
        [dot(everyone[:, t * hd : (t + 1) * hd], w_out).astype(BF16) for t in range(2)], axis=1
    )
    mixed = lax.psum_scatter(terms, "row", scatter_dimension=0, tiled=True)
    return (mixed.astype(F32) + flat.astype(F32)).astype(BF16).reshape(tokens.shape)


def solution(mesh):
    return jax.shard_map(
        body,
        mesh=mesh,
        in_specs=(
            P(("req", "row"), None, "col"),
            P("col", "row"),
            P("col", "row"),
            P("row", "col"),
            P("row", "col"),
            P(("req", "col"), None, "row"),
            P(("req", "col"), None, "row"),
            P(("req", "col")),
            P(("req", "col")),
            P(("req", "col"), "row"),
            P(("req", "col"), "row"),
            P(("req", "col")),
        ),
        out_specs=P(("req", "row"), None, "col"),
        check_vma=False,
    )
```
